128 devices in a mesh: section: 2 (over core), ctx: 16 (over x, y), tp: 4 (over z).
Axes of the slice: x: 4, y: 4, z: 4, core: 2. Of those that a mesh axis runs over, the one named last changes fastest.
Arguments:
- inputs: bfloat16 [2, 2048, 1024], P(None, 'ctx'), may hold values from -6 to 6
- positions: int32 [2, 2048], P(None, 'ctx'), may hold values from 0 to 1920, as said below
- cotangent: bfloat16 [2, 2048, 1024], P(None, 'ctx'), may hold values from -6 to 6
- attn_gain: bfloat16 [2, 1024], P('section', 'ctx'), may hold values from 0.099609375 to 1.8984375
- w_query: bfloat16 [2, 1024, 2048], P('section', 'ctx', 'tp'), may hold values from -0.1875 to 0.1875
- key_weight_matrix: bfloat16 [2, 1024, 1024], P('section', 'ctx', 'tp'), may hold values from -0.1875 to 0.1875
- value_weight_matrix: bfloat16 [2, 1024, 1024], P('section', 'ctx', 'tp'), may hold values from -0.1875 to 0.1875
- query_gain: bfloat16 [2, 128], P('section'), may hold values from 0.099609375 to 1.8984375
- key_gain: bfloat16 [2, 128], P('section'), may hold values from 0.099609375 to 1.8984375
- w_output: bfloat16 [2, 2048, 1024], P('section', 'tp', 'ctx'), may hold values from -0.75 to 0.75
- mlp_gain: bfloat16 [2, 1024], P('section', 'ctx'), may hold values from 0.099609375 to 1.8984375
- w_gate: bfloat16 [2, 1024, 3072], P('section', 'ctx', 'tp'), may hold values from -0.1875 to 0.1875
- w_up: bfloat16 [2, 1024, 3072], P('section', 'ctx', 'tp'), may hold values from -0.1875 to 0.1875
- w_down: bfloat16 [2, 3072, 1024], P('section', 'tp', 'ctx'), may hold values from -0.109375 to 0.109375
Outputs:
- section_out: bfloat16 [2, 2, 2048, 1024], P('section', None, 'ctx')
- input_grad: float32 [2, 2, 2048, 1024], P('section', None, 'ctx')
- g_attn_gain: float32 [2, 1024], P('section', 'ctx')
- g_query: float32 [2, 1024, 2048], P('section', 'ctx', 'tp')
- g_key: float32 [2, 1024, 1024], P('section', 'ctx', 'tp')
- g_value: float32 [2, 1024, 1024], P('section', 'ctx', 'tp')
- g_query_gain: float32 [2, 128], P('section')
- g_key_gain: float32 [2, 128], P('section')
- g_output: float32 [2, 2048, 1024], P('section', 'tp', 'ctx')
- g_mlp_gain: float32 [2, 1024], P('section', 'ctx')
- g_gate: float32 [2, 1024, 3072], P('section', 'ctx', 'tp')
- g_up: float32 [2, 1024, 3072], P('section', 'ctx', 'tp')
- g_down: float32 [2, 3072, 1024], P('section', 'tp', 'ctx')
The draws below stay inside these ranges and needn't reach their ends.
Inputs may be any that keep to these rules, and one draw needn't show every extreme that they name: `positions`: positions count the tokens of each packed document from 0 and rise by one from token to token; a document begins where the position is 0. In each micro-batch one document of 1921 tokens begins among the first 128 tokens and ends among the last 128.
All inputs are finite; a program needn't handle non-finite values.
Results may differ from the reference program's by a relative error of at most 0.034.
Values may be sent and summed in bfloat16 or wider, within the bound.
A program may use at most 128 MiB of HBM per device.

```python
import math
import jax
import jax.numpy as jnp
from jax import lax

MODEL_WIDTH = 1024
FF = 3072
QUERY_HEAD_COUNT = 16
KEY_VALUE_HEADS = 8
HEAD_SIZE = 128
MICRO = 2
SECTION_LAYERS = 2
SEQ = 2048
ROWS = 128


def draw_positions(key, part):
    key = jax.random.fold_in(key, 7)
    sub_keys = jax.random.split(key, 3)
    token_index = jnp.arange(SEQ, dtype=jnp.int32)[None, :]
    long_first = jax.random.randint(sub_keys[0], (MICRO, 1), 0, ROWS)
    long_last = long_first + (SEQ - ROWS)
    break_draw = jax.random.randint(sub_keys[2], (MICRO, SEQ), 0, 3) == 0
    outside = (token_index < long_first) | (token_index > long_last + 1)
    doc_start = (token_index == 0) | (token_index == long_first) | (token_index == long_last + 1) | break_draw & outside
    start_marks = jnp.where(doc_start, token_index, 0)
    return (token_index - lax.cummax(start_marks, axis=1)).astype(jnp.int32)


def with_spikes(values, own_key, source, target, blocks, factor):
    def block_of(dim):
        return (jnp.arange(values.shape[dim]) // (values.shape[dim] // blocks)).reshape((-1,) + (1,) * (values.ndim - 1 - dim))

    one_side = jax.random.permutation(own_key, blocks)[block_of(target)]
    other_side = (block_of(target) + blocks // 2) % blocks
    return jnp.where((block_of(source) == one_side) | (block_of(source) == other_side), factor * values, values)


def block_levels(rng, extent, cuts, smallest, largest):
    gain = 1.0
    for dim, blocks in cuts:
        draws = jax.random.uniform(jax.random.fold_in(jax.random.fold_in(rng, 6), dim), (blocks,), jnp.float32, smallest / len(cuts), largest / len(cuts))
        gain = gain * jnp.repeat(jnp.exp(draws), extent[dim] // blocks).reshape((-1,) + (1,) * (len(extent) - 1 - dim))
    return gain


def gaussian(key, dims, scale, reach, cuts=(), kind=jnp.bfloat16):
    entries = jax.random.normal(key, dims, jnp.float32) * scale
    if len(cuts) > 0:
        entries = block_levels(key, dims, cuts, -0.22, 0.18) * entries
    return jnp.clip(entries, min=-reach, max=reach).astype(kind)


def bell_draw_with(rng, shape, spread, most, cuts, heavy, kind=jnp.bfloat16):
    values = spread * jax.random.normal(rng, shape, jnp.float32)
    if cuts:
        values = values * block_levels(rng, shape, cuts, -0.22, 0.18)
    return jnp.clip(with_spikes(values, jax.random.fold_in(rng, 3), *heavy), -most, most).astype(kind)


def setup_inputs(seed: int = 0) -> dict:
    arg_keys = jax.random.split(jax.random.key(seed), 15)
    return {
        "inputs": bell_draw_with(arg_keys[0], (MICRO, SEQ, MODEL_WIDTH), 1.0, 6.0, ((1, 16),), (1, 2, 16, 2.0)),
        "positions": draw_positions(jax.random.fold_in(arg_keys[14], 71), 0),
        "cotangent": bell_draw_with(arg_keys[2], (MICRO, SEQ, MODEL_WIDTH), 1.0, 6.0, ((1, 16),), (1, 2, 16, 2.0)),
        "attn_gain": jnp.clip(1.0 + 0.18 * jax.random.normal(arg_keys[3], (SECTION_LAYERS, MODEL_WIDTH), jnp.float32), 0.099609375, 1.8984375).astype(jnp.bfloat16),
        "w_query": gaussian(arg_keys[4], (SECTION_LAYERS, MODEL_WIDTH, QUERY_HEAD_COUNT * HEAD_SIZE), MODEL_WIDTH ** -0.5, 0.1875, ((0, 2), (1, 16), (2, 4))),
        "key_weight_matrix": gaussian(arg_keys[5], (SECTION_LAYERS, MODEL_WIDTH, KEY_VALUE_HEADS * HEAD_SIZE), MODEL_WIDTH ** -0.5, 0.1875, ((0, 2), (1, 16), (2, 4))),
        "value_weight_matrix": gaussian(arg_keys[6], (SECTION_LAYERS, MODEL_WIDTH, KEY_VALUE_HEADS * HEAD_SIZE), MODEL_WIDTH ** -0.5, 0.1875, ((0, 2), (1, 16), (2, 4))),
        "query_gain": jnp.clip(1.0 + 0.18 * jax.random.normal(arg_keys[7], (SECTION_LAYERS, HEAD_SIZE), jnp.float32), 0.099609375, 1.8984375).astype(jnp.bfloat16),
        "key_gain": jnp.clip(1.0 + 0.18 * jax.random.normal(arg_keys[8], (SECTION_LAYERS, HEAD_SIZE), jnp.float32), 0.099609375, 1.8984375).astype(jnp.bfloat16),
        "w_output": gaussian(arg_keys[9], (SECTION_LAYERS, QUERY_HEAD_COUNT * HEAD_SIZE, MODEL_WIDTH), (max(1, 64 * QUERY_HEAD_COUNT * HEAD_SIZE // SEQ)) ** -0.5, 0.75, ((0, 2), (1, 4), (2, 16))),
        "mlp_gain": jnp.clip(1.0 + 0.18 * jax.random.normal(arg_keys[10], (SECTION_LAYERS, MODEL_WIDTH), jnp.float32), 0.099609375, 1.8984375).astype(jnp.bfloat16),
        "w_gate": gaussian(arg_keys[11], (SECTION_LAYERS, MODEL_WIDTH, FF), MODEL_WIDTH ** -0.5, 0.1875, ((0, 2), (1, 16), (2, 4))),
        "w_up": gaussian(arg_keys[12], (SECTION_LAYERS, MODEL_WIDTH, FF), MODEL_WIDTH ** -0.5, 0.1875, ((0, 2), (1, 16), (2, 4))),
        "w_down": gaussian(arg_keys[13], (SECTION_LAYERS, FF, MODEL_WIDTH), FF ** -0.5, 0.109375, ((0, 2), (1, 4), (2, 16))),
    }


EPSILON = 1e-06
ROPE_BASE = 1000000.0
PRECISE = lax.Precision.HIGHEST

@jax.custom_vjp
def reduced_input(v):
    return lax.optimization_barrier(v.astype(jnp.bfloat16)).astype(jnp.float32)

@jax.custom_vjp
def reduced_gradient(v):
    return v

def low_keep(v):
    return (reduced_input(v), None)

def low_pass(kept, grad):
    return (grad,)

def back_keep(v):
    return (v, None)

def back_low(kept, grad):
    return (reduced_input(grad),)
reduced_input.defvjp(low_keep, low_pass)
reduced_gradient.defvjp(back_keep, back_low)

def matrix_highprec(left_side, right_side):
    return jnp.dot(left_side, right_side, precision=PRECISE, preferred_element_type=jnp.float32)

def rms_scale(values, scale_gain):
    return values * lax.rsqrt(lax.optimization_barrier(jnp.mean(values * values, -1, keepdims=True)) + EPSILON) * scale_gain

def rotary(positions):
    half_dim = HEAD_SIZE // 2
    inv_freq = ROPE_BASE ** (-(jnp.arange(half_dim, dtype=jnp.float32) * 2.0 / HEAD_SIZE))
    angles = positions.astype(jnp.float32)[:, None] * inv_freq[None, :]
    return (jnp.cos(angles), jnp.sin(angles))

def apply_rope(values, cos_table, sin_table):
    half_dim = values.shape[-1] // 2
    lower_half = values[..., :half_dim]
    upper_half = values[..., half_dim:]
    cos_wide = cos_table[:, None, :]
    sin_wide = sin_table[:, None, :]
    return jnp.concatenate([lower_half * cos_wide - upper_half * sin_wide, upper_half * cos_wide + lower_half * sin_wide], -1)

def attention(query_rot, key_rot, value_projected, positions):
    sequence_length = query_rot.shape[0]
    query_group_width = QUERY_HEAD_COUNT // KEY_VALUE_HEADS
    score_scale = 1.0 / math.sqrt(HEAD_SIZE)
    key_heads = jnp.repeat(key_rot, query_group_width, axis=1)
    value_heads = jnp.repeat(value_projected, query_group_width, axis=1)
    token_index = jnp.arange(sequence_length, dtype=jnp.int32)
    doc_first = token_index - positions
    block_rows = math.gcd(sequence_length, 512)
    block_count = sequence_length // block_rows

    def one_block(pieces):
        query_block, block_index, block_first = pieces
        scores = reduced_gradient(jnp.einsum('qhd,khd->hqk', query_block, key_heads, precision=PRECISE) * score_scale)
        visible = (token_index[None, None, :] <= block_index[None, :, None]) & (token_index[None, None, :] >= block_first[None, :, None])
        scores = jnp.where(visible, scores, -1e+30)
        row_top = lax.optimization_barrier(jnp.max(scores, -1, keepdims=True))
        exp_scores = jnp.exp(scores - row_top)
        prob_low = reduced_input(exp_scores / lax.optimization_barrier(jnp.sum(exp_scores, -1, keepdims=True)))
        return jnp.einsum('hqk,khd->qhd', prob_low, value_heads, precision=PRECISE)
    outputs = lax.map(jax.checkpoint(one_block), (query_rot.reshape(block_count, block_rows, QUERY_HEAD_COUNT, HEAD_SIZE), token_index.reshape(block_count, block_rows), doc_first.reshape(block_count, block_rows)))
    return outputs.reshape(sequence_length, QUERY_HEAD_COUNT * HEAD_SIZE)

def layer_forward(layer_weight_set, hidden, positions):
    sequence_length = hidden.shape[0]
    normalized_state = reduced_input(rms_scale(hidden, layer_weight_set['attn_gain']))
    query_proj = reduced_gradient(matrix_highprec(normalized_state, layer_weight_set['w_query'])).reshape(sequence_length, QUERY_HEAD_COUNT, HEAD_SIZE)
    key_projected = reduced_gradient(matrix_highprec(normalized_state, layer_weight_set['w_key'])).reshape(sequence_length, KEY_VALUE_HEADS, HEAD_SIZE)
    value_projected = reduced_gradient(reduced_input(matrix_highprec(normalized_state, layer_weight_set['w_value']))).reshape(sequence_length, KEY_VALUE_HEADS, HEAD_SIZE)
    cos_table, sin_table = rotary(positions)
    query_rot = reduced_input(apply_rope(rms_scale(query_proj, layer_weight_set['query_gain']), cos_table, sin_table))
    key_rot = reduced_input(apply_rope(rms_scale(key_projected, layer_weight_set['key_gain']), cos_table, sin_table))
    mixed_out = reduced_gradient(reduced_input(attention(query_rot, key_rot, value_projected, positions)))
    after_attn = hidden + reduced_gradient(matrix_highprec(mixed_out, layer_weight_set['w_output']))
    mlp_in_low = reduced_input(rms_scale(after_attn, layer_weight_set['mlp_gain']))
    gate_proj = reduced_gradient(matrix_highprec(mlp_in_low, layer_weight_set['w_gate']))
    up_proj = reduced_gradient(matrix_highprec(mlp_in_low, layer_weight_set['w_up']))
    activated = reduced_input(jax.nn.silu(gate_proj) * up_proj)
    return after_attn + reduced_gradient(matrix_highprec(activated, layer_weight_set['w_down']))

def reference(inputs, positions, cotangent, attn_gain, w_query, key_weight_matrix, value_weight_matrix, query_gain, key_gain, w_output, mlp_gain, w_gate, w_up, w_down):
    arg_names = ['attn_gain', 'w_query', 'w_key', 'w_value', 'query_gain', 'key_gain', 'w_output', 'mlp_gain', 'w_gate', 'w_up', 'w_down']
    arg_list = [attn_gain, w_query, key_weight_matrix, value_weight_matrix, query_gain, key_gain, w_output, mlp_gain, w_gate, w_up, w_down]
    layer_weight_set = {key_name: leaf_arr.astype(jnp.float32) for key_name, leaf_arr in zip(arg_names, arg_list)}
    layer_count = attn_gain.shape[0]
    micro_count = inputs.shape[0]
    start_in = inputs.astype(jnp.float32)
    probes = jnp.zeros((micro_count, layer_count) + inputs.shape[1:], jnp.float32)

    def forward(layer_weight_set, start_in, probes):

        def per_micro(carry_in, pieces):
            hidden, probe_set, token_pos = pieces
            results = []
            for layer_id in range(layer_count):
                if layer_id > 0:
                    hidden = reduced_gradient(reduced_input(hidden))
                hidden = hidden + probe_set[layer_id]
                one_layer = jax.tree.map(lambda leaf_arr: leaf_arr[layer_id], layer_weight_set)
                hidden = layer_forward(one_layer, hidden, token_pos)
                results.append(hidden)
            return (carry_in, jnp.stack(results))
        carry_out, stacked = lax.scan(per_micro, jnp.zeros((), jnp.float32), (start_in, probes, positions))
        return stacked
    stacked, pullback = jax.vjp(forward, layer_weight_set, start_in, probes)
    cot_full = jnp.zeros_like(stacked).at[:, layer_count - 1].set(cotangent.astype(jnp.float32))
    grad_weights, unused_grad, grad_probes = pullback(cot_full)
    section_out = jnp.transpose(stacked, (1, 0, 2, 3)).astype(jnp.bfloat16)
    input_grad = jnp.transpose(grad_probes, (1, 0, 2, 3))
    return (section_out, input_grad, grad_weights['attn_gain'], grad_weights['w_query'], grad_weights['w_key'], grad_weights['w_value'], grad_weights['query_gain'], grad_weights['key_gain'], grad_weights['w_output'], grad_weights['mlp_gain'], grad_weights['w_gate'], grad_weights['w_up'], grad_weights['w_down'])
```

```python
import functools
import math

import jax
import jax.numpy as jnp
from jax import lax
from jax.experimental import pallas as pl
from jax.experimental.pallas import tpu as pltpu
from jax.sharding import PartitionSpec as P

HEAD_SIZE = 128
EPSILON = 1e-06
ROPE_BASE = 1000000.0
MASKED = -1e30
MESH = pl.DeviceIdType.MESH
BF = jnp.bfloat16
F32 = jnp.float32
CTX = 16
TP = 4
ROWS = 128
SUB = ROWS // TP
WIDTH = 1024
BLOCK = WIDTH // CTX
SIZES = (512, 256, 256, 768, 768, 512, 768)
STARTS = tuple(sum(SIZES[:n]) for n in range(len(SIZES) + 1))
PACK = STARTS[-1]
SCALE = 1.0 / math.sqrt(HEAD_SIZE)


def ring(axis, step, count):
    return lax.rem(lax.axis_index(axis) + step, count)


def remote(src, dst, send, recv, **where):
    return pltpu.make_async_remote_copy(
        src_ref=src, dst_ref=dst, send_sem=send, recv_sem=recv, device_id=where, device_id_type=MESH
    )


def greet(*groups):
    sem = pltpu.get_barrier_semaphore()
    total = 0
    for axis, count in groups:
        total += count - 1
        for step in range(1, count):
            pl.semaphore_signal(
                sem, inc=1, device_id={axis: ring(axis, step, count)}, device_id_type=MESH
            )
    pl.semaphore_wait(sem, total)


def params(collective_id, vmem=48):
    return pltpu.CompilerParams(
        collective_id=collective_id, has_side_effects=True, vmem_limit_bytes=vmem * 2**20
    )


VM = pl.BlockSpec(memory_space=pltpu.VMEM)
HB = pl.BlockSpec(memory_space=pl.ANY)
DMA = pltpu.SemaphoreType.DMA


def gather_weights_kernel(own, full, local, send, recv, pass_send, pass_recv):
    core = lax.axis_index("section")
    other = 1 - core
    here = lax.axis_index("ctx")
    greet(("ctx", CTX), ("section", 2))

    def spot(layer, index):
        return full.at[layer, pl.ds(pl.multiple_of(index * BLOCK, BLOCK), BLOCK)]

    mine = pltpu.make_async_copy(own, spot(core, here), local)
    mine.start()

    def out_copy(step):
        return remote(own, spot(core, here), send.at[step], recv.at[step], ctx=ring("ctx", step, CTX))

    def came(step):
        return ring("ctx", CTX - step, CTX)

    def pass_copy(step):
        source = spot(core, came(step))
        return remote(source, source, pass_send.at[step], pass_recv.at[step], section=other)

    first = remote(own, spot(core, here), pass_send.at[0], pass_recv.at[0], section=other)
    first.start()
    for step in range(1, CTX):
        out_copy(step).start()
    for step in range(1, CTX):
        place = spot(core, came(step))
        remote(place, place, send.at[step], recv.at[step], section=other).wait_recv()
        pass_copy(step).start()
    for step in range(CTX):
        place = spot(other, came(step) if step else here)
        remote(place, place, pass_send.at[step], pass_recv.at[step], section=other).wait_recv()
    mine.wait()
    first.wait_send()
    for step in range(1, CTX):
        out_copy(step).wait_send()
        pass_copy(step).wait_send()


def gather_weights(own):
    return pl.pallas_call(
        gather_weights_kernel,
        out_shape=jax.ShapeDtypeStruct((2, WIDTH, own.shape[1]), own.dtype),
        in_specs=[HB],
        out_specs=HB,
        scratch_shapes=[DMA, DMA((CTX,)), DMA((CTX,)), DMA((CTX,)), DMA((CTX,))],
        compiler_params=params(1),
    )(own)


def tp_rows(ref, index):
    return ref.at[pl.ds(pl.multiple_of(index * SUB, SUB), SUB)]


def tp_scatter_sum(part, landing, send, recv):
    here = lax.axis_index("tp")
    copies = []
    for step in range(1, TP):
        peer = ring("tp", step, TP)
        copies.append(
            remote(tp_rows(part, peer), landing.at[step - 1], send.at[step - 1], recv.at[step - 1], tp=peer)
        )
        copies[-1].start()
    total = tp_rows(part, here)[...].astype(F32)
    for step, copy in enumerate(copies):
        copy.wait_recv()
        total = total + landing[step].astype(F32)
    return total, copies


def tp_gather(full, send, recv):
    here = lax.axis_index("tp")
    copies = []
    for step in range(1, TP):
        peer = ring("tp", step, TP)
        place = tp_rows(full, here)
        copies.append(remote(place, place, send.at[step - 1], recv.at[step - 1], tp=peer))
        copies[-1].start()
    for step, copy in enumerate(copies):
        place = tp_rows(full, ring("tp", TP - 1 - step, TP))
        remote(place, place, send.at[step], recv.at[step], tp=here).wait_recv()
    return copies


TP_SCRATCH = [pltpu.VMEM((TP - 1, SUB, WIDTH), BF)] + [DMA((TP - 1,))] * 4


def finish(copies):
    for copy in copies:
        copy.wait_send()


def sum_norm_kernel(norm, part, resid, gain, new_resid, full, landing, s1, r1, s2, r2):
    greet(("tp", TP))
    total, sent = tp_scatter_sum(part, landing, s1, r1)
    total = total + resid[...]
    new_resid[...] = total
    if norm:
        total = total * lax.rsqrt(jnp.mean(total * total, -1, keepdims=True) + EPSILON) * gain[...]
    tp_rows(full, lax.axis_index("tp"))[...] = total.astype(BF)
    sent += tp_gather(full, s2, r2)
    finish(sent)


def sum_norm(part, resid, gain, norm, collective_id):
    return pl.pallas_call(
        functools.partial(sum_norm_kernel, norm),
        out_shape=(
            jax.ShapeDtypeStruct((SUB, WIDTH), F32),
            jax.ShapeDtypeStruct((ROWS, WIDTH), BF),
        ),
        in_specs=[VM] * 3,
        out_specs=(VM, VM),
        scratch_shapes=TP_SCRATCH,
        compiler_params=params(collective_id),
    )(part, resid, gain)


def norm_back(values, grad, gain):
    inverse = lax.rsqrt(jnp.mean(values * values, -1, keepdims=True) + EPSILON)
    unit = values * inverse
    scaled = grad * gain
    back = inverse * (scaled - unit * jnp.mean(scaled * unit, -1, keepdims=True))
    return back, jnp.sum(grad * unit, 0, keepdims=True)


def sum_back_kernel(part, values, resid_grad, gain, new_grad, full, gain_grad, landing, s1, r1, s2, r2):
    greet(("tp", TP))
    total, sent = tp_scatter_sum(part, landing, s1, r1)
    back, terms = norm_back(values[...], total, gain[...])
    gain_grad[...] = terms
    back = back + resid_grad[...]
    new_grad[...] = back
    tp_rows(full, lax.axis_index("tp"))[...] = back.astype(BF)
    sent += tp_gather(full, s2, r2)
    finish(sent)


def sum_back(part, values, resid_grad, gain, collective_id):
    return pl.pallas_call(
        sum_back_kernel,
        out_shape=(
            jax.ShapeDtypeStruct((SUB, WIDTH), F32),
            jax.ShapeDtypeStruct((ROWS, WIDTH), BF),
            jax.ShapeDtypeStruct((1, WIDTH), F32),
        ),
        in_specs=[VM] * 4,
        out_specs=(VM, VM, VM),
        scratch_shapes=TP_SCRATCH,
        compiler_params=params(collective_id),
    )(part, values, resid_grad, gain)


def ctx_rows(ref, index):
    return ref.at[pl.ds(pl.multiple_of(index * ROWS, ROWS), ROWS)]


def gather_keys_kernel(own, full, local, send, recv):
    here = lax.axis_index("ctx")
    greet(("ctx", CTX))
    mine = pltpu.make_async_copy(own, ctx_rows(full, here), local)
    mine.start()

    def out_copy(step):
        return remote(own, ctx_rows(full, here), send.at[step], recv.at[step], ctx=ring("ctx", step, CTX))

    for step in range(1, CTX):
        out_copy(step).start()
    for step in range(1, CTX):
        place = ctx_rows(full, ring("ctx", CTX - step, CTX))
        remote(place, place, send.at[step], recv.at[step], ctx=here).wait_recv()
    mine.wait()
    for step in range(1, CTX):
        out_copy(step).wait_send()


def gather_keys(own, collective_id):
    return pl.pallas_call(
        gather_keys_kernel,
        out_shape=jax.ShapeDtypeStruct((CTX * ROWS, own.shape[1]), BF),
        in_specs=[VM],
        out_specs=VM,
        scratch_shapes=[DMA, DMA((CTX,)), DMA((CTX,))],
        compiler_params=params(collective_id),
    )(own)


def scatter_keys_kernel(part, total, landing, send, recv):
    here = lax.axis_index("ctx")
    greet(("ctx", CTX))

    def out_copy(step):
        peer = ring("ctx", step, CTX)
        return remote(ctx_rows(part, peer), landing.at[step - 1], send.at[step], recv.at[step], ctx=peer)

    for step in range(1, CTX):
        out_copy(step).start()
    total[...] = ctx_rows(part, here)[...].astype(F32)
    for step in range(1, CTX):
        out_copy(step).wait_recv()
        total[...] += landing[step - 1].astype(F32)
    for step in range(1, CTX):
        out_copy(step).wait_send()


def scatter_keys(part, collective_id):
    return pl.pallas_call(
        scatter_keys_kernel,
        out_shape=jax.ShapeDtypeStruct((ROWS, part.shape[1]), F32),
        in_specs=[VM],
        out_specs=VM,
        scratch_shapes=[
            pltpu.VMEM((CTX - 1, ROWS, part.shape[1]), BF),
            DMA((CTX,)),
            DMA((CTX,)),
        ],
        compiler_params=params(collective_id),
    )(part)


def scatter_grads_kernel(
    grads, small, acts, inner, total, small_total, acts_other, inner_other,
    mine, theirs, landing, small_theirs, small_sum, small_land, small_part, small_tp,
    local, pair_send, pair_recv, send, recv, ss, sr, cs, cr, ts, tr, es, er,
):
    core = lax.axis_index("section")
    other = 1 - core
    here = lax.axis_index("ctx")
    greet(("ctx", CTX), ("section", 2), ("tp", TP))

    def rows(ref, index):
        return ref.at[pl.ds(pl.multiple_of(index * BLOCK, BLOCK), BLOCK)]

    def pair_copy(step):
        peer = ring("ctx", step, CTX)
        return remote(
            rows(grads.at[other], peer), rows(theirs, peer), pair_send.at[step], pair_recv.at[step], section=other
        )

    def load(step):
        peer = ring("ctx", step, CTX)
        return pltpu.make_async_copy(rows(grads.at[core], peer), rows(mine, peer), local.at[step])

    def out_copy(step):
        peer = ring("ctx", step, CTX)
        return remote(rows(mine, peer), landing.at[step - 1], send.at[step], recv.at[step], ctx=peer)

    swaps = [
        remote(small.at[other], small_theirs, ss.at[0], sr.at[0], section=other),
        remote(acts.at[other], acts_other, es.at[0], er.at[0], section=other),
        remote(inner.at[other], inner_other, es.at[1], er.at[1], section=other),
    ]
    swaps[0].start()
    order = [*range(1, CTX), 0]
    for step in order:
        pair_copy(step).start()
        load(step).start()
    swaps[1].start()
    swaps[2].start()
    swaps[0].wait_recv()
    small_sum[...] = small[core] + small_theirs[...]

    def small_copy(step):
        peer = ring("ctx", step, CTX)
        return remote(small_sum.at[peer], small_land.at[step - 1], cs.at[step], cr.at[step], ctx=peer)

    for step in range(1, CTX):
        small_copy(step).start()
    for step in order:
        load(step).wait()
        pair_copy(step).wait_recv()
        peer = ring("ctx", step, CTX)
        rows(mine, peer)[...] = (
            rows(mine, peer)[...].astype(F32) + rows(theirs, peer)[...].astype(F32)
        ).astype(BF)
        if step:
            out_copy(step).start()
    part = small_sum[here]
    for step in range(1, CTX):
        small_copy(step).wait_recv()
        part = part + small_land[step - 1]
    small_part[...] = part
    tp_copies = []
    for step in range(1, TP):
        tp_copies.append(
            remote(small_part, small_tp.at[step - 1], ts.at[step - 1], tr.at[step - 1], tp=ring("tp", step, TP))
        )
        tp_copies[-1].start()
    total[...] = rows(mine, here)[...].astype(F32)
    for step in range(1, CTX):
        out_copy(step).wait_recv()
        total[...] += landing[step - 1].astype(F32)
    for step, copy in enumerate(tp_copies):
        copy.wait_recv()
        part = part + small_tp[step]
    small_total[...] = part
    swaps[1].wait_recv()
    swaps[2].wait_recv()
    for copy in swaps + tp_copies:
        copy.wait_send()
    for step in range(CTX):
        pair_copy(step).wait_send()
        if step:
            out_copy(step).wait_send()
            small_copy(step).wait_send()


def scatter_grads(grads, small, acts, inner):
    tile = (8, 128)
    return pl.pallas_call(
        scatter_grads_kernel,
        out_shape=(
            jax.ShapeDtypeStruct((BLOCK, PACK), F32),
            jax.ShapeDtypeStruct(tile, F32),
            jax.ShapeDtypeStruct((ROWS, WIDTH), BF),
            jax.ShapeDtypeStruct((ROWS, WIDTH), BF),
        ),
        in_specs=[HB, VM, HB, HB],
        out_specs=(VM, VM, HB, HB),
        scratch_shapes=[
            pltpu.VMEM((WIDTH, PACK), BF),
            pltpu.VMEM((WIDTH, PACK), BF),
            pltpu.VMEM((CTX - 1, BLOCK, PACK), BF),
            pltpu.VMEM((CTX, *tile), F32),
            pltpu.VMEM((CTX, *tile), F32),
            pltpu.VMEM((CTX - 1, *tile), F32),
            pltpu.VMEM(tile, F32),
            pltpu.VMEM((TP - 1, *tile), F32),
            DMA((CTX,)), DMA((CTX,)), DMA((CTX,)), DMA((CTX,)), DMA((CTX,)),
            DMA((1,)), DMA((1,)), DMA((CTX,)), DMA((CTX,)),
            DMA((TP - 1,)), DMA((TP - 1,)), DMA((2,)), DMA((2,)),
        ],
        compiler_params=params(2),
    )(grads, small, acts, inner)


def rms_scale(values, scale_gain):
    return values * lax.rsqrt(jnp.mean(values * values, -1, keepdims=True) + EPSILON) * scale_gain


def rotary(positions):
    half_dim = HEAD_SIZE // 2
    inv_freq = ROPE_BASE ** (-(jnp.arange(half_dim, dtype=F32) * 2.0 / HEAD_SIZE))
    angles = positions.astype(F32)[:, None] * inv_freq[None, :]
    return (jnp.cos(angles), jnp.sin(angles))


def apply_rope(values, cos_table, sin_table):
    half_dim = values.shape[-1] // 2
    lower_half = values[..., :half_dim]
    upper_half = values[..., half_dim:]
    cos_wide = cos_table[:, None, :]
    sin_wide = sin_table[:, None, :]
    return jnp.concatenate(
        [
            lower_half * cos_wide - upper_half * sin_wide,
            upper_half * cos_wide + lower_half * sin_wide,
        ],
        -1,
    )


def rope_norm(values, scale_gain, cos_table, sin_table):
    row_count = values.shape[0]
    head_view = values.reshape(row_count, -1, HEAD_SIZE)
    return apply_rope(rms_scale(head_view, scale_gain), cos_table, sin_table).reshape(row_count, -1)


def swiglu(gate_proj, up_proj):
    return jax.nn.silu(gate_proj) * up_proj


def dot(a, b, contract):
    return lax.dot_general(a, b, ((contract[:1], contract[1:]), ((), ())), preferred_element_type=F32)


def visible_mask(token_index, doc_first):
    columns = jnp.arange(CTX * ROWS, dtype=jnp.int32)
    return (columns[None, :] <= token_index[:, None]) & (columns[None, :] >= doc_first[:, None])


def attend(query, keys, values, visible):
    query = query.reshape(ROWS, 2, 2, HEAD_SIZE)
    keys = keys.reshape(-1, 2, HEAD_SIZE)
    values = values.reshape(-1, 2, HEAD_SIZE)
    scores = jnp.einsum("rkgd,skd->kgrs", query, keys, preferred_element_type=F32) * SCALE
    scores = jnp.where(visible, scores, MASKED)
    top = jnp.max(scores, -1, keepdims=True)
    raised = jnp.exp(scores - top)
    total = jnp.sum(raised, -1, keepdims=True)
    low = (raised / total).astype(BF)
    mixed = jnp.einsum("kgrs,skd->rkgd", low, values, preferred_element_type=F32)
    return mixed.reshape(ROWS, -1).astype(BF), top, total


def attend_back(query, keys, values, visible, top, total, grad):
    query = query.reshape(ROWS, 2, 2, HEAD_SIZE)
    grad = grad.reshape(ROWS, 2, 2, HEAD_SIZE)
    keys = keys.reshape(-1, 2, HEAD_SIZE)
    values = values.reshape(-1, 2, HEAD_SIZE)
    scores = jnp.einsum("rkgd,skd->kgrs", query, keys, preferred_element_type=F32) * SCALE
    prob = jnp.exp(jnp.where(visible, scores, MASKED) - top) / total
    prob_grad = jnp.einsum("rkgd,skd->kgrs", grad, values, preferred_element_type=F32)
    row_dot = jnp.sum(prob * prob_grad, -1, keepdims=True)
    low = (prob * (prob_grad - row_dot)).astype(BF)
    query_grad = jnp.einsum("kgrs,skd->rkgd", low, keys, preferred_element_type=F32) * SCALE
    key_grad = jnp.einsum("kgrs,rkgd->skd", low, query, preferred_element_type=F32) * SCALE
    value_grad = jnp.einsum("kgrs,rkgd->skd", prob.astype(BF), grad, preferred_element_type=F32)
    return query_grad.reshape(ROWS, -1), key_grad.reshape(-1, 256), value_grad.reshape(-1, 256)


def own_rows(full):
    return lax.dynamic_slice_in_dim(full, lax.axis_index("tp") * SUB, SUB, 0).astype(F32)


def layer_forward(w, hidden, tables, visible, ids):
    normed = rms_scale(hidden.astype(F32), w["attn_gain"]).astype(BF)
    query_proj = dot(normed, w["query"], (1, 0))
    key_proj = dot(normed, w["key"], (1, 0))
    value = dot(normed, w["value"], (1, 0)).astype(BF)
    query = rope_norm(query_proj, w["query_gain"], *tables).astype(BF)
    key = rope_norm(key_proj, w["key_gain"], *tables).astype(BF)
    both = gather_keys(jnp.concatenate([key, value], 1), ids[0])
    keys, values = both[:, :256], both[:, 256:]
    mixed, top, total = attend(query, keys, values, visible)
    part = dot(mixed, w["output"], (1, 1)).astype(BF)
    after, mlp_in = sum_norm(part, own_rows(hidden), w["mlp_gain"], True, ids[1])
    gate = dot(mlp_in, w["gate"], (1, 0))
    up = dot(mlp_in, w["up"], (1, 0))
    activated = swiglu(gate, up).astype(BF)
    part = dot(activated, w["down"], (1, 1)).astype(BF)
    result = sum_norm(part, after, w["mlp_gain"], False, ids[2])[1]
    stash = dict(
        hidden=hidden, normed=normed, query_proj=query_proj, key_proj=key_proj, query=query, keys=keys,
        values=values, top=top, total=total, mixed=mixed, after=after, mlp_in=mlp_in, gate=gate, up=up,
        activated=activated,
    )
    return result, stash


def layer_backward(w, s, grad_rows, grad_low, tables, visible, ids):
    g_down = dot(grad_low, s["activated"], (0, 0))
    act_grad = dot(grad_low, w["down"], (1, 0))
    gate_grad, up_grad = jax.vjp(swiglu, s["gate"], s["up"])[1](act_grad)
    gate_low, up_low = gate_grad.astype(BF), up_grad.astype(BF)
    g_gate = dot(s["mlp_in"], gate_low, (0, 0))
    g_up = dot(s["mlp_in"], up_low, (0, 0))
    part = dot(gate_low, w["gate"], (1, 1)) + dot(up_low, w["up"], (1, 1))
    grad_rows, grad_low, g_mlp_gain = sum_back(part.astype(BF), s["after"], grad_rows, w["mlp_gain"], ids[0])
    g_output = dot(grad_low, s["mixed"], (0, 0))
    mixed_grad = dot(grad_low, w["output"], (1, 0)).astype(BF)
    query_grad, key_all, value_all = attend_back(
        s["query"], s["keys"], s["values"], visible, s["top"], s["total"], mixed_grad
    )
    both = scatter_keys(jnp.concatenate([key_all, value_all], 1).astype(BF), ids[1])
    key_grad, value_low = both[:, :256], both[:, 256:].astype(BF)
    turned = lambda v, g: rope_norm(v, g, *tables)
    query_grad, g_query_gain = jax.vjp(turned, s["query_proj"], w["query_gain"])[1](query_grad)
    key_grad, g_key_gain = jax.vjp(turned, s["key_proj"], w["key_gain"])[1](key_grad)
    query_low, key_low = query_grad.astype(BF), key_grad.astype(BF)
    joined = jnp.concatenate([query_low, key_low, value_low], 1)
    g_first = dot(s["normed"], joined, (0, 0))
    part = dot(joined, w["first"], (1, 1))
    grad_rows, grad_low, g_attn_gain = sum_back(
        part.astype(BF), own_rows(s["hidden"]), grad_rows, w["attn_gain"], ids[2]
    )
    packed = jnp.concatenate([g_first, g_gate, g_up, g_output, g_down], 1).astype(BF)
    gains = jnp.concatenate([g_attn_gain.reshape(CTX, 1, BLOCK), g_mlp_gain.reshape(CTX, 1, BLOCK)], 2)
    heads = jnp.stack([g_query_gain, g_key_gain])[None]
    small = jnp.concatenate(
        [gains, jnp.broadcast_to(heads, (CTX, 2, 128)), jnp.zeros((CTX, 5, 128), F32)], 1
    )
    return grad_rows, grad_low, packed, small


def on_device(
    inputs, positions, cotangent, attn_gain, w_query, w_key, w_value, query_gain, key_gain, w_output,
    mlp_gain, w_gate, w_up, w_down,
):
    core = lax.axis_index("section")
    hidden = lax.dynamic_index_in_dim(inputs, core, 0, keepdims=False)
    token_pos = lax.dynamic_index_in_dim(positions, core, 0, keepdims=False)
    top_grad = lax.dynamic_index_in_dim(cotangent, core, 0, keepdims=False)
    gains = jnp.concatenate(
        [attn_gain.T, mlp_gain.T, jnp.broadcast_to(query_gain, (BLOCK, 128))[:, :0]], 1
    )
    heads = jnp.concatenate([query_gain, key_gain], 0).reshape(4, BLOCK).T
    gains = jnp.concatenate([gains, heads, jnp.zeros((BLOCK, 122), BF)], 1)
    own = jnp.concatenate(
        [w_query[0], w_key[0], w_value[0], w_gate[0], w_up[0], w_output[0].T, w_down[0].T, gains], 1
    )
    full = gather_weights(own)
    weights = []
    names = ("query", "key", "value", "gate", "up", "output", "down")
    for layer in range(2):
        w = {
            name: full[layer, :, STARTS[n] : STARTS[n + 1]] for n, name in enumerate(names)
        }
        w["first"] = full[layer, :, :1024]
        tail = full[layer, :, PACK : PACK + 8].astype(F32)
        w["attn_gain"] = tail[:, 0][None]
        w["mlp_gain"] = tail[:, 1][None]
        heads = tail[:BLOCK, 2:6].T.reshape(2, 128)
        w["query_gain"], w["key_gain"] = heads[0], heads[1]
        weights.append(w)
    token_index = lax.axis_index("ctx") * ROWS + jnp.arange(ROWS, dtype=jnp.int32)
    tables = rotary(token_pos)
    visible = visible_mask(token_index, token_index - token_pos)
    outs, stashes = [], []
    for layer in range(2):
        hidden, stash = layer_forward(weights[layer], hidden, tables, visible, [3 + 3 * layer + n for n in range(3)])
        outs.append(hidden)
        stashes.append(stash)
    grad_low = top_grad
    grad_rows = own_rows(top_grad)
    grads, smalls, inner = [None] * 2, [None] * 2, [None] * 2
    for layer in (1, 0):
        grad_rows, grad_low, grads[layer], smalls[layer] = layer_backward(
            weights[layer], stashes[layer], grad_rows, grad_low, tables, visible, [9 + 3 * layer + n for n in range(3)]
        )
        inner[layer] = grad_low
        grad_rows = own_rows(grad_low)
    acts, inner = jnp.stack(outs), jnp.stack(inner)
    total, small, acts_other, inner_other = scatter_grads(jnp.stack(grads), jnp.stack(smalls), acts, inner)

    def both_micros(stacked, received):
        own = lax.dynamic_index_in_dim(stacked, core, 0, keepdims=False)
        low, high = jnp.where(core == 0, own, received), jnp.where(core == 0, received, own)
        return jnp.stack([low, high])[None]

    cut = [total[:, STARTS[n] : STARTS[n + 1]] for n in range(7)]
    return (
        both_micros(acts, acts_other),
        both_micros(inner, inner_other).astype(F32),
        small[0, :BLOCK][None],
        cut[0][None],
        cut[1][None],
        cut[2][None],
        small[1][None],
        small[2][None],
        cut[5].T[None],
        small[0, BLOCK:][None],
        cut[3][None],
        cut[4][None],
        cut[6].T[None],
    )


def solution(mesh):
    row, col = P("section", "ctx", "tp"), P("section", "tp", "ctx")
    gain, head = P("section", "ctx"), P("section", None)
    tokens = P(None, "ctx", None)
    layered = P("section", None, "ctx", None)
    return jax.shard_map(
        on_device,
        mesh=mesh,
        in_specs=(tokens, P(None, "ctx"), tokens, gain, row, row, row, head, head, col, gain, row, row, col),
        out_specs=(layered, layered, gain, row, row, row, head, head, col, gain, row, row, col),
        check_vma=False,
    )
```

```python
import functools
import math

import jax
import jax.numpy as jnp
from jax import lax
from jax.experimental import pallas as pl
from jax.experimental.pallas import tpu as pltpu
from jax.sharding import PartitionSpec as P

HEAD_SIZE = 128
EPSILON = 1e-06
ROPE_BASE = 1000000.0
MASKED = -1e30
MESH = pl.DeviceIdType.MESH
BF = jnp.bfloat16
F32 = jnp.float32
CTX = 16
TP = 4
ROWS = 128
SUB = ROWS // TP
WIDTH = 1024
BLOCK = WIDTH // CTX
SIZES = (512, 256, 256, 768, 768, 512, 768)
STARTS = tuple(sum(SIZES[:n]) for n in range(len(SIZES) + 1))
PACK = STARTS[-1]
SCALE = 1.0 / math.sqrt(HEAD_SIZE)


def ring(axis, step, count):
    return lax.rem(lax.axis_index(axis) + step, count)


def remote(src, dst, send, recv, **where):
    return pltpu.make_async_remote_copy(
        src_ref=src, dst_ref=dst, send_sem=send, recv_sem=recv, device_id=where, device_id_type=MESH
    )


def greet(*groups):
    sem = pltpu.get_barrier_semaphore()
    total = 0
    for axis, count in groups:
        total += count - 1
        for step in range(1, count):
            pl.semaphore_signal(
                sem, inc=1, device_id={axis: ring(axis, step, count)}, device_id_type=MESH
            )
    pl.semaphore_wait(sem, total)


def params(collective_id, vmem=48):
    return pltpu.CompilerParams(
        collective_id=collective_id, has_side_effects=True, vmem_limit_bytes=vmem * 2**20
    )


VM = pl.BlockSpec(memory_space=pltpu.VMEM)
HB = pl.BlockSpec(memory_space=pl.ANY)
DMA = pltpu.SemaphoreType.DMA


EDGE = 4
HEADS = 4
FIRST = 1280
REST = 2816
GATE, UP, OUT, DOWN = 0, 768, 1536, 2048
HALF = {FIRST: (384, 256), REST: (768, 640)}


def place():
    here = lax.axis_index("ctx")
    return here // EDGE, lax.rem(here, EDGE)


def around(value, step):
    return lax.rem(value + step, EDGE)


def peer_x(step):
    x, y = place()
    return around(x, step) * EDGE + y


def peer_y(step):
    x, y = place()
    return x * EDGE + around(y, step)


def greet_plane():
    sem = pltpu.get_barrier_semaphore()
    for step in range(1, EDGE):
        for where in ({"ctx": peer_x(step)}, {"ctx": peer_y(step)}, {"tp": ring("tp", step, TP)}):
            pl.semaphore_signal(sem, inc=1, device_id=where, device_id_type=MESH)
    pl.semaphore_signal(
        sem, inc=1, device_id={"section": 1 - lax.axis_index("section")}, device_id_type=MESH
    )
    pl.semaphore_wait(sem, 3 * (EDGE - 1) + 1)


class PlaneGather:
    def __init__(self, ref, cols_a, cols_b, send, recv):
        self.ref, self.a, self.b, self.send, self.recv = ref, cols_a, cols_b, send, recv
        self.sent = []

    def push(self, src, slot, peer):
        copy = remote(src, src, self.send.at[slot], self.recv.at[slot], ctx=peer)
        copy.start()
        self.sent.append(copy)

    def wait(self, dst, slot):
        remote(dst, dst, self.send.at[slot], self.recv.at[slot], ctx=lax.axis_index("ctx")).wait_recv()

    def start(self):
        x, y = place()
        for step in range(1, EDGE):
            self.push(self.ref.at[x, y, :, self.a], step - 1, peer_x(step))
            self.push(self.ref.at[x, y, :, self.b], step + 2, peer_y(step))

    def middle(self):
        x, y = place()
        for step in range(1, EDGE):
            self.wait(self.ref.at[around(x, EDGE - step), y, :, self.a], step - 1)
        for step in range(1, EDGE):
            self.push(self.ref.at[:, y, :, self.a], step + 5, peer_y(step))
        for step in range(1, EDGE):
            self.wait(self.ref.at[x, around(y, EDGE - step), :, self.b], step + 2)
        for step in range(1, EDGE):
            self.push(self.ref.at[x, :, :, self.b], step + 8, peer_x(step))

    def second(self):
        x, y = place()
        for step in range(1, EDGE):
            yield self.ref.at[:, around(y, EDGE - step), :, self.a], step + 5
            yield self.ref.at[around(x, EDGE - step), :, :, self.b], step + 8

    def end(self):
        for dst, slot in self.second():
            self.wait(dst, slot)

    def finish(self):
        finish(self.sent)


class WeightGather(PlaneGather):
    def __init__(self, ref, send, recv, pair_send, pair_recv):
        width = ref.shape[-1]
        first, second = HALF[width]

        def cols(core):
            low = pl.multiple_of(core * (width // 2), 128)
            return pl.ds(low, first), pl.ds(pl.multiple_of(low + first, 128), second)

        core = lax.axis_index("section")
        super().__init__(ref, *cols(core), send, recv)
        self.theirs = cols(1 - core)
        self.pair_send, self.pair_recv = pair_send, pair_recv

    def hand(self, src, slot):
        other = 1 - lax.axis_index("section")
        copy = remote(src, src, self.pair_send.at[slot], self.pair_recv.at[slot], section=other)
        copy.start()
        self.sent.append(copy)

    def taken(self, dst, slot):
        here = lax.axis_index("section")
        remote(dst, dst, self.pair_send.at[slot], self.pair_recv.at[slot], section=here).wait_recv()

    def middle(self):
        super().middle()
        x, y = place()
        self.hand(self.ref.at[:, y, :, self.a], 0)
        self.hand(self.ref.at[x, :, :, self.b], 1)

    def end(self):
        x, y = place()
        for n, (dst, slot) in enumerate(self.second()):
            self.wait(dst, slot)
            self.hand(dst, n + 2)
        a, b = self.theirs
        self.taken(self.ref.at[:, y, :, a], 0)
        self.taken(self.ref.at[x, :, :, b], 1)
        for step in range(1, EDGE):
            self.taken(self.ref.at[:, around(y, EDGE - step), :, a], 2 * step)
            self.taken(self.ref.at[around(x, EDGE - step), :, :, b], 2 * step + 1)


def mm(a, b, contract=(1, 0)):
    return lax.dot_general(a, b, (((contract[0],), (contract[1],)), ((), ())), preferred_element_type=F32)


def flat(ref, layer, low, size):
    value = ref[layer, :, :, :, low : low + size]
    return value.reshape(-1, size)


def unit_rms(values):
    return values * lax.rsqrt(jnp.mean(values * values, -1, keepdims=True) + EPSILON)


def head(value, index):
    return value[:, index * HEAD_SIZE : (index + 1) * HEAD_SIZE]


def turn(values, gain, cos, sin):
    outs = []
    for index in range(values.shape[1] // HEAD_SIZE):
        scaled = unit_rms(head(values, index)) * gain
        outs.append(scaled * cos + pltpu.roll(scaled, HEAD_SIZE // 2, 1) * sin)
    return jnp.concatenate(outs, 1).astype(BF)


def scores_t(keys, query, first):
    raw = mm(keys, query, (1, 1)) * SCALE
    rows = lax.broadcasted_iota(jnp.int32, raw.shape, 0)
    last = lax.axis_index("ctx") * ROWS + lax.broadcasted_iota(jnp.int32, (1, ROWS), 1)
    return jnp.where((rows <= last) & (rows >= first), raw, MASKED)


def forward_layer(layer, hidden, w1, w2, first, cos, sin, st, tp_sems, keys_gather, mid_keys, mid_out, mid_mlp):
    here = lax.axis_index("tp")
    x, y = place()
    gains = flat(w1, layer, 1024, 128).astype(F32).T[:8]
    st["gains"][layer] = gains
    heads = w1[layer, 0, 0, 0:16, 1152:1280].astype(F32)
    st["head_gains"][layer] = heads[:8]
    normed = (unit_rms(hidden[...].astype(F32)) * gains[0:1]).astype(BF)
    st["normed"][layer] = normed
    query_proj = mm(normed, flat(w1, layer, 0, 512))
    key_proj = mm(normed, flat(w1, layer, 512, 256))
    value = mm(normed, flat(w1, layer, 768, 256))
    st["query_proj"][layer] = query_proj
    st["key_proj"][layer] = key_proj
    kv = st["kv"]
    kv[layer, x, y, :, 0:256] = turn(key_proj, heads[1:2], cos, sin)
    kv[layer, x, y, :, 256:512] = value.astype(BF)
    keys_gather.start()
    query = turn(query_proj, heads[0:1], cos, sin)
    st["query"][layer] = query
    keys_gather.middle()
    mid_keys()
    keys_gather.end()
    mixed = []
    for group in range(2):
        keys = flat(kv, layer, group * HEAD_SIZE, HEAD_SIZE)
        values_t = flat(kv, layer, 256 + group * HEAD_SIZE, HEAD_SIZE).T
        for index in (2 * group, 2 * group + 1):
            scores = scores_t(keys, head(query, index), first)
            top = jnp.max(scores, 0, keepdims=True)
            raised = jnp.exp(scores - top)
            total = jnp.sum(raised, 0, keepdims=True)
            low = (raised * (1.0 / total)).astype(BF)
            st["level"][layer, index : index + 1, :] = top + jnp.log(total)
            mixed.append(mm(values_t, low).T.astype(BF))
    mixed = jnp.concatenate(mixed, 1)
    st["mixed"][layer] = mixed
    mid_out()
    part, landing = st["part"], st["landing"]
    part[2 * layer] = mm(mixed, flat(w2, layer, OUT, 512), (1, 1)).astype(BF)
    sems = [s.at[2 * layer] for s in tp_sems]
    total, sent = tp_scatter_sum(part.at[2 * layer], landing.at[2 * layer], sems[0], sems[1])
    after = total + hidden[pl.ds(pl.multiple_of(here * SUB, SUB), SUB), :].astype(F32)
    st["after"][layer] = after
    mlp_in = st["mlp_in"].at[layer]
    tp_rows(mlp_in, here)[...] = (unit_rms(after) * gains[1:2]).astype(BF)
    sent += tp_gather(mlp_in, sems[2], sems[3])
    mid_mlp()
    gate = mm(mlp_in[...], flat(w2, layer, GATE, 768))
    up = mm(mlp_in[...], flat(w2, layer, UP, 768))
    st["gate"][layer] = gate
    st["up"][layer] = up
    activated = (gate / (1.0 + jnp.exp(-gate)) * up).astype(BF)
    part[2 * layer + 1] = mm(activated, flat(w2, layer, DOWN, 768), (1, 1)).astype(BF)
    sems = [s.at[2 * layer + 1] for s in tp_sems]
    total, sent2 = tp_scatter_sum(part.at[2 * layer + 1], landing.at[2 * layer + 1], sems[0], sems[1])
    out = st["outs"].at[layer]
    tp_rows(out, here)[...] = (total + after).astype(BF)
    sent2 += tp_gather(out, sems[2], sems[3])
    return sent + sent2


STASH = dict(
    kv=((2, EDGE, EDGE, ROWS, 512), BF),
    normed=((2, ROWS, WIDTH), BF),
    query_proj=((2, ROWS, 512), F32),
    key_proj=((2, ROWS, 256), F32),
    query=((2, ROWS, 512), BF),
    level=((2, 8, ROWS), F32),
    mixed=((2, ROWS, 512), BF),
    after=((2, SUB, WIDTH), F32),
    mlp_in=((2, ROWS, WIDTH), BF),
    gate=((2, ROWS, 768), F32),
    up=((2, ROWS, 768), F32),
    outs=((2, ROWS, WIDTH), BF),
    gains=((2, 8, WIDTH), F32),
    head_gains=((2, 8, HEAD_SIZE), F32),
)
WEIGHTS = [((2, EDGE, EDGE, BLOCK, FIRST), BF), ((2, EDGE, EDGE, BLOCK, REST), BF)]


def forward_kernel(own1, own2, inputs, first, cos, sin, w1, w2, *refs):
    st = dict(zip(STASH, refs))
    refs = refs[len(STASH) :]
    st["part"], st["landing"] = refs[:2]
    tp_sems, (local, swap_send, swap_recv, send, recv, pair_send, pair_recv, kv_send, kv_recv) = refs[2:6], refs[6:]
    core = lax.axis_index("section")
    other = 1 - core
    x, y = place()
    gathers = [
        [
            WeightGather(ref.at[layer], send.at[2 * layer + n], recv.at[2 * layer + n],
                         pair_send.at[2 * layer + n], pair_recv.at[2 * layer + n])
            for n, ref in enumerate((w1, w2))
        ]
        for layer in range(2)
    ]
    greet_plane()
    swaps, locals_ = [], []
    for n, (own, ref) in enumerate(((own1, w1), (own2, w2))):
        half = own.shape[1] // 2
        cut = pl.ds(pl.multiple_of(other * half, 128), half)
        keep = pl.ds(pl.multiple_of(core * half, 128), half)
        swaps.append(remote(own.at[:, cut], ref.at[core, x, y, :, cut], swap_send.at[n], swap_recv.at[n], section=other))
        swaps[-1].start()
        locals_.append(pltpu.make_async_copy(own.at[:, keep], ref.at[core, x, y, :, keep], local.at[n]))
        locals_[-1].start()
    for n, ref in enumerate((w1, w2)):
        half = ref.shape[-1] // 2
        keep = pl.ds(pl.multiple_of(core * half, 128), half)
        dst = ref.at[other, x, y, :, keep]
        locals_[n].wait()
        remote(dst, dst, swap_send.at[n], swap_recv.at[n], section=core).wait_recv()
        if n == 0:
            gathers[0][0].start()
    gathers[0][0].middle()
    gathers[0][1].start()
    gathers[0][0].end()
    keys = [
        PlaneGather(st["kv"].at[layer], pl.ds(0, 256), pl.ds(256, 256), kv_send.at[layer], kv_recv.at[layer])
        for layer in range(2)
    ]

    def mid_keys_first():
        gathers[0][1].middle()

    def mid_out_first():
        gathers[0][1].end()
        gathers[1][0].start()

    def mid_mlp_first():
        gathers[1][0].middle()
        gathers[1][1].start()

    def mid_keys_second():
        gathers[1][1].end()

    hidden = inputs.at[core]
    sent = forward_layer(0, hidden, w1, w2, first[...], cos[...], sin[...], st, tp_sems, keys[0], mid_keys_first, mid_out_first, mid_mlp_first)
    gathers[1][1].middle()
    gathers[1][0].end()
    hidden = st["outs"].at[0]
    sent += forward_layer(1, hidden, w1, w2, first[...], cos[...], sin[...], st, tp_sems, keys[1], mid_keys_second, lambda: None, lambda: None)
    finish(sent + swaps)
    for part in keys + gathers[0] + gathers[1]:
        part.finish()


def run_forward(own1, own2, inputs, first, cos, sin):
    outs = WEIGHTS + list(STASH.values())
    return pl.pallas_call(
        forward_kernel,
        out_shape=[jax.ShapeDtypeStruct(*o) for o in outs],
        in_specs=[VM] * 6,
        out_specs=[VM] * len(outs),
        scratch_shapes=[
            pltpu.VMEM((4, ROWS, WIDTH), BF),
            pltpu.VMEM((4, TP - 1, SUB, WIDTH), BF),
            *[DMA((4, TP - 1))] * 4,
            DMA((2,)), DMA((2,)), DMA((2,)),
            DMA((4, 12)), DMA((4, 12)), DMA((4, 8)), DMA((4, 8)), DMA((2, 12)), DMA((2, 12)),
        ],
        compiler_params=params(1, 60),
    )(own1, own2, inputs, first, cos, sin)


def tp_rows(ref, index):
    return ref.at[pl.ds(pl.multiple_of(index * SUB, SUB), SUB)]


def tp_scatter_sum(part, landing, send, recv):
    here = lax.axis_index("tp")
    copies = []
    for step in range(1, TP):
        peer = ring("tp", step, TP)
        copies.append(
            remote(tp_rows(part, peer), landing.at[step - 1], send.at[step - 1], recv.at[step - 1], tp=peer)
        )
        copies[-1].start()
    total = tp_rows(part, here)[...].astype(F32)
    for step, copy in enumerate(copies):
        copy.wait_recv()
        total = total + landing[step].astype(F32)
    return total, copies


def tp_gather(full, send, recv):
    here = lax.axis_index("tp")
    copies = []
    for step in range(1, TP):
        peer = ring("tp", step, TP)
        place = tp_rows(full, here)
        copies.append(remote(place, place, send.at[step - 1], recv.at[step - 1], tp=peer))
        copies[-1].start()
    for step, copy in enumerate(copies):
        place = tp_rows(full, ring("tp", TP - 1 - step, TP))
        remote(place, place, send.at[step], recv.at[step], tp=here).wait_recv()
    return copies


TP_SCRATCH = [pltpu.VMEM((TP - 1, SUB, WIDTH), BF)] + [DMA((TP - 1,))] * 4


def finish(copies):
    for copy in copies:
        copy.wait_send()


def norm_back(values, grad, gain):
    inverse = lax.rsqrt(jnp.mean(values * values, -1, keepdims=True) + EPSILON)
    unit = values * inverse
    scaled = grad * gain
    back = inverse * (scaled - unit * jnp.mean(scaled * unit, -1, keepdims=True))
    return back, jnp.sum(grad * unit, 0, keepdims=True)


def sum_back_kernel(part, values, resid_grad, gain, new_grad, full, gain_grad, landing, s1, r1, s2, r2):
    greet(("tp", TP))
    total, sent = tp_scatter_sum(part, landing, s1, r1)
    back, terms = norm_back(values[...], total, gain[...])
    gain_grad[...] = terms
    back = back + resid_grad[...]
    new_grad[...] = back
    tp_rows(full, lax.axis_index("tp"))[...] = back.astype(BF)
    sent += tp_gather(full, s2, r2)
    finish(sent)


def sum_back(part, values, resid_grad, gain, collective_id):
    return pl.pallas_call(
        sum_back_kernel,
        out_shape=(
            jax.ShapeDtypeStruct((SUB, WIDTH), F32),
            jax.ShapeDtypeStruct((ROWS, WIDTH), BF),
            jax.ShapeDtypeStruct((1, WIDTH), F32),
        ),
        in_specs=[VM] * 4,
        out_specs=(VM, VM, VM),
        scratch_shapes=TP_SCRATCH,
        compiler_params=params(collective_id),
    )(part, values, resid_grad, gain)


def ctx_rows(ref, index):
    return ref.at[pl.ds(pl.multiple_of(index * ROWS, ROWS), ROWS)]


def scatter_keys_kernel(part, total, landing, send, recv):
    here = lax.axis_index("ctx")
    greet(("ctx", CTX))

    def out_copy(step):
        peer = ring("ctx", step, CTX)
        return remote(ctx_rows(part, peer), landing.at[step - 1], send.at[step], recv.at[step], ctx=peer)

    for step in range(1, CTX):
        out_copy(step).start()
    total[...] = ctx_rows(part, here)[...].astype(F32)
    for step in range(1, CTX):
        out_copy(step).wait_recv()
        total[...] += landing[step - 1].astype(F32)
    for step in range(1, CTX):
        out_copy(step).wait_send()


def scatter_keys(part, collective_id):
    return pl.pallas_call(
        scatter_keys_kernel,
        out_shape=jax.ShapeDtypeStruct((ROWS, part.shape[1]), F32),
        in_specs=[VM],
        out_specs=VM,
        scratch_shapes=[
            pltpu.VMEM((CTX - 1, ROWS, part.shape[1]), BF),
            DMA((CTX,)),
            DMA((CTX,)),
        ],
        compiler_params=params(collective_id),
    )(part)


def scatter_grads_kernel(
    grads, small, acts, inner, total, small_total, acts_other, inner_other,
    mine, theirs, landing, small_theirs, small_sum, small_land, small_part, small_tp,
    local, pair_send, pair_recv, send, recv, ss, sr, cs, cr, ts, tr, es, er,
):
    core = lax.axis_index("section")
    other = 1 - core
    here = lax.axis_index("ctx")
    greet(("ctx", CTX), ("section", 2), ("tp", TP))

    def rows(ref, index):
        return ref.at[pl.ds(pl.multiple_of(index * BLOCK, BLOCK), BLOCK)]

    def pair_copy(step):
        peer = ring("ctx", step, CTX)
        return remote(
            rows(grads.at[other], peer), rows(theirs, peer), pair_send.at[step], pair_recv.at[step], section=other
        )

    def load(step):
        peer = ring("ctx", step, CTX)
        return pltpu.make_async_copy(rows(grads.at[core], peer), rows(mine, peer), local.at[step])

    def out_copy(step):
        peer = ring("ctx", step, CTX)
        return remote(rows(mine, peer), landing.at[step - 1], send.at[step], recv.at[step], ctx=peer)

    swaps = [
        remote(small.at[other], small_theirs, ss.at[0], sr.at[0], section=other),
        remote(acts.at[other], acts_other, es.at[0], er.at[0], section=other),
        remote(inner.at[other], inner_other, es.at[1], er.at[1], section=other),
    ]
    swaps[0].start()
    order = [*range(1, CTX), 0]
    for step in order:
        pair_copy(step).start()
        load(step).start()
    swaps[1].start()
    swaps[2].start()
    swaps[0].wait_recv()
    small_sum[...] = small[core] + small_theirs[...]

    def small_copy(step):
        peer = ring("ctx", step, CTX)
        return remote(small_sum.at[peer], small_land.at[step - 1], cs.at[step], cr.at[step], ctx=peer)

    for step in range(1, CTX):
        small_copy(step).start()
    for step in order:
        load(step).wait()
        pair_copy(step).wait_recv()
        peer = ring("ctx", step, CTX)
        rows(mine, peer)[...] = (
            rows(mine, peer)[...].astype(F32) + rows(theirs, peer)[...].astype(F32)
        ).astype(BF)
        if step:
            out_copy(step).start()
    part = small_sum[here]
    for step in range(1, CTX):
        small_copy(step).wait_recv()
        part = part + small_land[step - 1]
    small_part[...] = part
    tp_copies = []
    for step in range(1, TP):
        tp_copies.append(
            remote(small_part, small_tp.at[step - 1], ts.at[step - 1], tr.at[step - 1], tp=ring("tp", step, TP))
        )
        tp_copies[-1].start()
    total[...] = rows(mine, here)[...].astype(F32)
    for step in range(1, CTX):
        out_copy(step).wait_recv()
        total[...] += landing[step - 1].astype(F32)
    for step, copy in enumerate(tp_copies):
        copy.wait_recv()
        part = part + small_tp[step]
    small_total[...] = part
    swaps[1].wait_recv()
    swaps[2].wait_recv()
    for copy in swaps + tp_copies:
        copy.wait_send()
    for step in range(CTX):
        pair_copy(step).wait_send()
        if step:
            out_copy(step).wait_send()
            small_copy(step).wait_send()


def scatter_grads(grads, small, acts, inner):
    tile = (8, 128)
    return pl.pallas_call(
        scatter_grads_kernel,
        out_shape=(
            jax.ShapeDtypeStruct((BLOCK, PACK), F32),
            jax.ShapeDtypeStruct(tile, F32),
            jax.ShapeDtypeStruct((ROWS, WIDTH), BF),
            jax.ShapeDtypeStruct((ROWS, WIDTH), BF),
        ),
        in_specs=[HB, VM, HB, HB],
        out_specs=(VM, VM, HB, HB),
        scratch_shapes=[
            pltpu.VMEM((WIDTH, PACK), BF),
            pltpu.VMEM((WIDTH, PACK), BF),
            pltpu.VMEM((CTX - 1, BLOCK, PACK), BF),
            pltpu.VMEM((CTX, *tile), F32),
            pltpu.VMEM((CTX, *tile), F32),
            pltpu.VMEM((CTX - 1, *tile), F32),
            pltpu.VMEM(tile, F32),
            pltpu.VMEM((TP - 1, *tile), F32),
            DMA((CTX,)), DMA((CTX,)), DMA((CTX,)), DMA((CTX,)), DMA((CTX,)),
            DMA((1,)), DMA((1,)), DMA((CTX,)), DMA((CTX,)),
            DMA((TP - 1,)), DMA((TP - 1,)), DMA((2,)), DMA((2,)),
        ],
        compiler_params=params(2),
    )(grads, small, acts, inner)


def rms_scale(values, scale_gain):
    return values * lax.rsqrt(jnp.mean(values * values, -1, keepdims=True) + EPSILON) * scale_gain


def rotary(positions):
    half_dim = HEAD_SIZE // 2
    inv_freq = ROPE_BASE ** (-(jnp.arange(half_dim, dtype=F32) * 2.0 / HEAD_SIZE))
    angles = positions.astype(F32)[:, None] * inv_freq[None, :]
    return (jnp.cos(angles), jnp.sin(angles))


def apply_rope(values, cos_table, sin_table):
    half_dim = values.shape[-1] // 2
    lower_half = values[..., :half_dim]
    upper_half = values[..., half_dim:]
    cos_wide = cos_table[:, None, :]
    sin_wide = sin_table[:, None, :]
    return jnp.concatenate(
        [
            lower_half * cos_wide - upper_half * sin_wide,
            upper_half * cos_wide + lower_half * sin_wide,
        ],
        -1,
    )


def rope_norm(values, scale_gain, cos_table, sin_table):
    row_count = values.shape[0]
    head_view = values.reshape(row_count, -1, HEAD_SIZE)
    return apply_rope(rms_scale(head_view, scale_gain), cos_table, sin_table).reshape(row_count, -1)


def swiglu(gate_proj, up_proj):
    return jax.nn.silu(gate_proj) * up_proj


def dot(a, b, contract):
    return lax.dot_general(a, b, ((contract[:1], contract[1:]), ((), ())), preferred_element_type=F32)


def visible_mask(token_index, doc_first):
    columns = jnp.arange(CTX * ROWS, dtype=jnp.int32)
    return (columns[None, :] <= token_index[:, None]) & (columns[None, :] >= doc_first[:, None])


def attend_back(query, keys, values, visible, top, total, grad):
    query = query.reshape(ROWS, 2, 2, HEAD_SIZE)
    grad = grad.reshape(ROWS, 2, 2, HEAD_SIZE)
    keys = keys.reshape(-1, 2, HEAD_SIZE)
    values = values.reshape(-1, 2, HEAD_SIZE)
    scores = jnp.einsum("rkgd,skd->kgrs", query, keys, preferred_element_type=F32) * SCALE
    prob = jnp.exp(jnp.where(visible, scores, MASKED) - top) / total
    prob_grad = jnp.einsum("rkgd,skd->kgrs", grad, values, preferred_element_type=F32)
    row_dot = jnp.sum(prob * prob_grad, -1, keepdims=True)
    low = (prob * (prob_grad - row_dot)).astype(BF)
    query_grad = jnp.einsum("kgrs,skd->rkgd", low, keys, preferred_element_type=F32) * SCALE
    key_grad = jnp.einsum("kgrs,rkgd->skd", low, query, preferred_element_type=F32) * SCALE
    value_grad = jnp.einsum("kgrs,rkgd->skd", prob.astype(BF), grad, preferred_element_type=F32)
    return query_grad.reshape(ROWS, -1), key_grad.reshape(-1, 256), value_grad.reshape(-1, 256)


def own_rows(full):
    return lax.dynamic_slice_in_dim(full, lax.axis_index("tp") * SUB, SUB, 0).astype(F32)


def layer_backward(w, s, grad_rows, grad_low, tables, visible, ids):
    g_down = dot(grad_low, s["activated"], (0, 0))
    act_grad = dot(grad_low, w["down"], (1, 0))
    gate_grad, up_grad = jax.vjp(swiglu, s["gate"], s["up"])[1](act_grad)
    gate_low, up_low = gate_grad.astype(BF), up_grad.astype(BF)
    g_gate = dot(s["mlp_in"], gate_low, (0, 0))
    g_up = dot(s["mlp_in"], up_low, (0, 0))
    part = dot(gate_low, w["gate"], (1, 1)) + dot(up_low, w["up"], (1, 1))
    grad_rows, grad_low, g_mlp_gain = sum_back(part.astype(BF), s["after"], grad_rows, w["mlp_gain"], ids[0])
    g_output = dot(grad_low, s["mixed"], (0, 0))
    mixed_grad = dot(grad_low, w["output"], (1, 0)).astype(BF)
    query_grad, key_all, value_all = attend_back(
        s["query"], s["keys"], s["values"], visible, s["top"], s["total"], mixed_grad
    )
    both = scatter_keys(jnp.concatenate([key_all, value_all], 1).astype(BF), ids[1])
    key_grad, value_low = both[:, :256], both[:, 256:].astype(BF)
    turned = lambda v, g: rope_norm(v, g, *tables)
    query_grad, g_query_gain = jax.vjp(turned, s["query_proj"], w["query_gain"])[1](query_grad)
    key_grad, g_key_gain = jax.vjp(turned, s["key_proj"], w["key_gain"])[1](key_grad)
    query_low, key_low = query_grad.astype(BF), key_grad.astype(BF)
    joined = jnp.concatenate([query_low, key_low, value_low], 1)
    g_first = dot(s["normed"], joined, (0, 0))
    part = dot(joined, w["first"], (1, 1))
    grad_rows, grad_low, g_attn_gain = sum_back(
        part.astype(BF), own_rows(s["hidden"]), grad_rows, w["attn_gain"], ids[2]
    )
    packed = jnp.concatenate([g_first, g_gate, g_up, g_output, g_down], 1).astype(BF)
    gains = jnp.concatenate([g_attn_gain.reshape(CTX, 1, BLOCK), g_mlp_gain.reshape(CTX, 1, BLOCK)], 2)
    heads = jnp.stack([g_query_gain, g_key_gain])[None]
    small = jnp.concatenate(
        [gains, jnp.broadcast_to(heads, (CTX, 2, 128)), jnp.zeros((CTX, 5, 128), F32)], 1
    )
    return grad_rows, grad_low, packed, small


def wide_tables(token_pos):
    cos, sin = rotary(token_pos)
    return jnp.concatenate([cos, cos], 1), jnp.concatenate([-sin, sin], 1)


def on_device(
    inputs, positions, cotangent, attn_gain, w_query, w_key, w_value, query_gain, key_gain, w_output,
    mlp_gain, w_gate, w_up, w_down,
):
    core = lax.axis_index("section")
    token_pos = lax.dynamic_index_in_dim(positions, core, 0, keepdims=False)
    top_grad = lax.dynamic_index_in_dim(cotangent, core, 0, keepdims=False)
    gains = jnp.concatenate([attn_gain.T, mlp_gain.T, jnp.zeros((BLOCK, 126), BF)], 1)
    heads = jnp.concatenate([query_gain, key_gain, jnp.zeros((BLOCK - 2, 128), BF)], 0)
    own1 = jnp.concatenate([w_query[0], w_key[0], w_value[0], gains, heads], 1)
    own2 = jnp.concatenate([w_gate[0], w_up[0], w_output[0].T, w_down[0].T], 1)
    token_index = lax.axis_index("ctx") * ROWS + jnp.arange(ROWS, dtype=jnp.int32)
    tables = rotary(token_pos)
    first = token_index - token_pos
    w1, w2, *stash = run_forward(own1, own2, inputs, first[None], *wide_tables(token_pos))
    st = dict(zip(STASH, stash))
    w1, w2 = w1.reshape(2, WIDTH, FIRST), w2.reshape(2, WIDTH, REST)
    st["kv"] = st["kv"].reshape(2, CTX * ROWS, 512)
    visible = visible_mask(token_index, first)
    grad_low = top_grad
    grad_rows = own_rows(top_grad)
    grads, smalls, inner = [None] * 2, [None] * 2, [None] * 2
    for layer in (1, 0):
        w = dict(
            first=w1[layer, :, :1024], gate=w2[layer, :, GATE : GATE + 768], up=w2[layer, :, UP : UP + 768],
            output=w2[layer, :, OUT : OUT + 512], down=w2[layer, :, DOWN : DOWN + 768],
            attn_gain=st["gains"][layer, 0:1], mlp_gain=st["gains"][layer, 1:2],
            query_gain=st["head_gains"][layer, 0], key_gain=st["head_gains"][layer, 1],
        )
        s = {name: value[layer] for name, value in st.items()}
        s["keys"], s["values"] = s["kv"][:, :256], s["kv"][:, 256:]
        s["hidden"] = st["outs"][0] if layer else lax.dynamic_index_in_dim(inputs, core, 0, keepdims=False)
        s["top"] = s["level"][:4].reshape(2, 2, ROWS, 1)
        s["total"] = jnp.ones((), F32)
        s["activated"] = swiglu(s["gate"], s["up"]).astype(BF)
        grad_rows, grad_low, grads[layer], smalls[layer] = layer_backward(
            w, s, grad_rows, grad_low, tables, visible, [9 + 3 * layer + n for n in range(3)]
        )
        inner[layer] = grad_low
        grad_rows = own_rows(grad_low)
    acts, inner = st["outs"], jnp.stack(inner)
    total, small, acts_other, inner_other = scatter_grads(jnp.stack(grads), jnp.stack(smalls), acts, inner)

    def both_micros(stacked, received):
        own = lax.dynamic_index_in_dim(stacked, core, 0, keepdims=False)
        low, high = jnp.where(core == 0, own, received), jnp.where(core == 0, received, own)
        return jnp.stack([low, high])[None]

    cut = [total[:, STARTS[n] : STARTS[n + 1]] for n in range(7)]
    return (
        both_micros(acts, acts_other),
        both_micros(inner, inner_other).astype(F32),
        small[0, :BLOCK][None],
        cut[0][None],
        cut[1][None],
        cut[2][None],
        small[1][None],
        small[2][None],
        cut[5].T[None],
        small[0, BLOCK:][None],
        cut[3][None],
        cut[4][None],
        cut[6].T[None],
    )


def solution(mesh):
    row, col = P("section", "ctx", "tp"), P("section", "tp", "ctx")
    gain, head = P("section", "ctx"), P("section", None)
    tokens = P(None, "ctx", None)
    layered = P("section", None, "ctx", None)
    return jax.shard_map(
        on_device,
        mesh=mesh,
        in_specs=(tokens, P(None, "ctx"), tokens, gain, row, row, row, head, head, col, gain, row, row, col),
        out_specs=(layered, layered, gain, row, row, row, head, head, col, gain, row, row, col),
        check_vma=False,
    )
```

```python
import math

import jax
import jax.numpy as jnp
from jax import lax
from jax.experimental import pallas as pl
from jax.experimental.pallas import tpu as pltpu
from jax.sharding import PartitionSpec as P

HEAD_SIZE = 128
EPSILON = 1e-06
ROPE_BASE = 1000000.0
MASKED = -1e30
MESH = pl.DeviceIdType.MESH
BF = jnp.bfloat16
F32 = jnp.float32
CTX = 16
TP = 4
ROWS = 128
SUB = ROWS // TP
WIDTH = 1024
BLOCK = WIDTH // CTX
SCALE = 1.0 / math.sqrt(HEAD_SIZE)


def ring(axis, step, count):
    return lax.rem(lax.axis_index(axis) + step, count)


def remote(src, dst, send, recv, **where):
    return pltpu.make_async_remote_copy(
        src_ref=src, dst_ref=dst, send_sem=send, recv_sem=recv, device_id=where, device_id_type=MESH
    )


def params(collective_id, vmem=48):
    return pltpu.CompilerParams(
        collective_id=collective_id, has_side_effects=True, vmem_limit_bytes=vmem * 2**20
    )


VM = pl.BlockSpec(memory_space=pltpu.VMEM)
HB = pl.BlockSpec(memory_space=pl.ANY)
DMA = pltpu.SemaphoreType.DMA


EDGE = 4
HEADS = 4
FIRST = 1280
REST = 2816
GATE, UP, OUT, DOWN = 0, 768, 1536, 2048
HALF = {FIRST: (384, 256), REST: (768, 640)}


def place():
    here = lax.axis_index("ctx")
    return here // EDGE, lax.rem(here, EDGE)


def around(value, step):
    return lax.rem(value + step, EDGE)


def peer_x(step):
    x, y = place()
    return around(x, step) * EDGE + y


def peer_y(step):
    x, y = place()
    return x * EDGE + around(y, step)


def greet_plane():
    sem = pltpu.get_barrier_semaphore()
    for step in range(1, EDGE):
        for where in ({"ctx": peer_x(step)}, {"ctx": peer_y(step)}, {"tp": ring("tp", step, TP)}):
            pl.semaphore_signal(sem, inc=1, device_id=where, device_id_type=MESH)
    pl.semaphore_signal(
        sem, inc=1, device_id={"section": 1 - lax.axis_index("section")}, device_id_type=MESH
    )
    pl.semaphore_wait(sem, 3 * (EDGE - 1) + 1)


class PlaneGather:
    def __init__(self, ref, cols_a, cols_b, send, recv):
        self.ref, self.a, self.b, self.send, self.recv = ref, cols_a, cols_b, send, recv
        self.sent = []

    def push(self, src, slot, peer):
        copy = remote(src, src, self.send.at[slot], self.recv.at[slot], ctx=peer)
        copy.start()
        self.sent.append(copy)

    def wait(self, dst, slot):
        remote(dst, dst, self.send.at[slot], self.recv.at[slot], ctx=lax.axis_index("ctx")).wait_recv()

    def start(self):
        x, y = place()
        for step in range(1, EDGE):
            self.push(self.ref.at[x, y, :, self.a], step - 1, peer_x(step))
            self.push(self.ref.at[x, y, :, self.b], step + 2, peer_y(step))

    def middle(self):
        x, y = place()
        for step in range(1, EDGE):
            self.wait(self.ref.at[around(x, EDGE - step), y, :, self.a], step - 1)
        for step in range(1, EDGE):
            self.push(self.ref.at[:, y, :, self.a], step + 5, peer_y(step))
        for step in range(1, EDGE):
            self.wait(self.ref.at[x, around(y, EDGE - step), :, self.b], step + 2)
        for step in range(1, EDGE):
            self.push(self.ref.at[x, :, :, self.b], step + 8, peer_x(step))

    def second(self):
        x, y = place()
        for step in range(1, EDGE):
            yield self.ref.at[:, around(y, EDGE - step), :, self.a], step + 5
            yield self.ref.at[around(x, EDGE - step), :, :, self.b], step + 8

    def end(self):
        for dst, slot in self.second():
            self.wait(dst, slot)

    def finish(self):
        finish(self.sent)


class WeightGather(PlaneGather):
    def __init__(self, ref, send, recv, pair_send, pair_recv):
        width = ref.shape[-1]
        first, second = HALF[width]

        def cols(core):
            low = pl.multiple_of(core * (width // 2), 128)
            return pl.ds(low, first), pl.ds(pl.multiple_of(low + first, 128), second)

        core = lax.axis_index("section")
        super().__init__(ref, *cols(core), send, recv)
        self.theirs = cols(1 - core)
        self.pair_send, self.pair_recv = pair_send, pair_recv

    def hand(self, src, slot):
        other = 1 - lax.axis_index("section")
        copy = remote(src, src, self.pair_send.at[slot], self.pair_recv.at[slot], section=other)
        copy.start()
        self.sent.append(copy)

    def taken(self, dst, slot):
        here = lax.axis_index("section")
        remote(dst, dst, self.pair_send.at[slot], self.pair_recv.at[slot], section=here).wait_recv()

    def middle(self):
        super().middle()
        x, y = place()
        self.hand(self.ref.at[:, y, :, self.a], 0)
        self.hand(self.ref.at[x, :, :, self.b], 1)

    def end(self):
        x, y = place()
        for n, (dst, slot) in enumerate(self.second()):
            self.wait(dst, slot)
            self.hand(dst, n + 2)
        a, b = self.theirs
        self.taken(self.ref.at[:, y, :, a], 0)
        self.taken(self.ref.at[x, :, :, b], 1)
        for step in range(1, EDGE):
            self.taken(self.ref.at[:, around(y, EDGE - step), :, a], 2 * step)
            self.taken(self.ref.at[around(x, EDGE - step), :, :, b], 2 * step + 1)


def mm(a, b, contract=(1, 0)):
    return lax.dot_general(a, b, (((contract[0],), (contract[1],)), ((), ())), preferred_element_type=F32)


def flat(ref, layer, low, size):
    value = ref[layer, :, :, :, low : low + size]
    return value.reshape(-1, size)


def unit_rms(values):
    return values * lax.rsqrt(jnp.mean(values * values, -1, keepdims=True) + EPSILON)


def head(value, index):
    return value[:, index * HEAD_SIZE : (index + 1) * HEAD_SIZE]


def turn(values, gain, cos, sin):
    outs = []
    for index in range(values.shape[1] // HEAD_SIZE):
        scaled = unit_rms(head(values, index)) * gain
        outs.append(scaled * cos + pltpu.roll(scaled, HEAD_SIZE // 2, 1) * sin)
    return jnp.concatenate(outs, 1).astype(BF)


def scores_t(keys, query, first):
    raw = mm(keys, query, (1, 1)) * SCALE
    rows = lax.broadcasted_iota(jnp.int32, raw.shape, 0)
    last = lax.axis_index("ctx") * ROWS + lax.broadcasted_iota(jnp.int32, (1, ROWS), 1)
    return jnp.where((rows <= last) & (rows >= first), raw, MASKED)


def forward_layer(layer, hidden, w1, w2, first, cos, sin, st, tp_sems, keys_gather, mid_keys, mid_out, mid_mlp):
    here = lax.axis_index("tp")
    x, y = place()
    gains = flat(w1, layer, 1024, 128).astype(F32).T[:8]
    st["gains"][layer] = gains
    heads = w1[layer, 0, 0, 0:16, 1152:1280].astype(F32)
    st["head_gains"][layer] = heads[:8]
    normed = (unit_rms(hidden[...].astype(F32)) * gains[0:1]).astype(BF)
    st["normed"][layer] = normed
    query_proj = mm(normed, flat(w1, layer, 0, 512))
    key_proj = mm(normed, flat(w1, layer, 512, 256))
    value = mm(normed, flat(w1, layer, 768, 256))
    st["query_proj"][layer] = query_proj
    st["key_proj"][layer] = key_proj
    kv = st["kv"]
    kv[layer, x, y, :, 0:256] = turn(key_proj, heads[1:2], cos, sin)
    kv[layer, x, y, :, 256:512] = value.astype(BF)
    keys_gather.start()
    query = turn(query_proj, heads[0:1], cos, sin)
    st["query"][layer] = query
    keys_gather.middle()
    mid_keys()
    keys_gather.end()
    st["keep_kv"](layer)
    mixed = []
    for group in range(2):
        keys = flat(kv, layer, group * HEAD_SIZE, HEAD_SIZE)
        values_t = flat(kv, layer, 256 + group * HEAD_SIZE, HEAD_SIZE).T
        for index in (2 * group, 2 * group + 1):
            scores = scores_t(keys, head(query, index), first)
            top = jnp.max(scores, 0, keepdims=True)
            raised = jnp.exp(scores - top)
            total = jnp.sum(raised, 0, keepdims=True)
            low = (raised * (1.0 / total)).astype(BF)
            st["level"][layer, index : index + 1, :] = top + jnp.log(total)
            mixed.append(mm(values_t, low).T.astype(BF))
    mixed = jnp.concatenate(mixed, 1)
    st["mixed"][layer] = mixed
    mid_out()
    part, landing = st["part"], st["landing"]
    part[2 * layer] = mm(mixed, flat(w2, layer, OUT, 512), (1, 1)).astype(BF)
    sems = [s.at[2 * layer] for s in tp_sems]
    total, sent = tp_scatter_sum(part.at[2 * layer], landing.at[2 * layer], sems[0], sems[1])
    after = total + hidden[pl.ds(pl.multiple_of(here * SUB, SUB), SUB), :].astype(F32)
    st["after"][layer] = after
    mlp_in = st["mlp_in"].at[layer]
    tp_rows(mlp_in, here)[...] = (unit_rms(after) * gains[1:2]).astype(BF)
    sent += tp_gather(mlp_in, sems[2], sems[3])
    mid_mlp()
    gate = mm(mlp_in[...], flat(w2, layer, GATE, 768))
    up = mm(mlp_in[...], flat(w2, layer, UP, 768))
    st["gate"][layer] = gate
    st["up"][layer] = up
    activated = (gate / (1.0 + jnp.exp(-gate)) * up).astype(BF)
    part[2 * layer + 1] = mm(activated, flat(w2, layer, DOWN, 768), (1, 1)).astype(BF)
    sems = [s.at[2 * layer + 1] for s in tp_sems]
    total, sent2 = tp_scatter_sum(part.at[2 * layer + 1], landing.at[2 * layer + 1], sems[0], sems[1])
    out = st["outs"].at[layer]
    tp_rows(out, here)[...] = (total + after).astype(BF)
    sent2 += tp_gather(out, sems[2], sems[3])
    return sent + sent2


STASH = dict(
    normed=((2, ROWS, WIDTH), BF),
    query_proj=((2, ROWS, 512), F32),
    key_proj=((2, ROWS, 256), F32),
    query=((2, ROWS, 512), BF),
    level=((2, 8, ROWS), F32),
    mixed=((2, ROWS, 512), BF),
    after=((2, SUB, WIDTH), F32),
    mlp_in=((2, ROWS, WIDTH), BF),
    gate=((2, ROWS, 768), F32),
    up=((2, ROWS, 768), F32),
    outs=((2, ROWS, WIDTH), BF),
    gains=((2, 8, WIDTH), F32),
    head_gains=((2, 8, HEAD_SIZE), F32),
)
KEPT = [
    ((2, EDGE, EDGE, BLOCK, FIRST), BF),
    ((2, EDGE, EDGE, BLOCK, REST), BF),
    ((2, EDGE, EDGE, ROWS, 512), BF),
]


def forward_kernel(own1, own2, inputs, first, cos, sin, w1_out, w2_out, kv_out, outs_other, *refs):
    st = dict(zip(STASH, refs))
    w1, w2, st["kv"], st["part"], st["landing"], *refs = refs[len(STASH) :]
    tp_sems, (local, swap_send, swap_recv, send, recv, pair_send, pair_recv, kv_send, kv_recv, keep) = refs[:4], refs[4:]
    core = lax.axis_index("section")
    other = 1 - core
    x, y = place()
    kept = []

    def keep_copy(src, dst, layer, n):
        kept.append(pltpu.make_async_copy(src.at[layer], dst.at[layer], keep.at[layer, n]))
        kept[-1].start()

    st["keep_kv"] = lambda layer: keep_copy(st["kv"], kv_out, layer, 2)
    gathers = [
        [
            WeightGather(ref.at[layer], send.at[2 * layer + n], recv.at[2 * layer + n],
                         pair_send.at[2 * layer + n], pair_recv.at[2 * layer + n])
            for n, ref in enumerate((w1, w2))
        ]
        for layer in range(2)
    ]

    def complete(layer, n):
        gathers[layer][n].end()
        keep_copy((w1, w2)[n], (w1_out, w2_out)[n], layer, n)

    greet_plane()
    swaps, locals_ = [], []
    for n, (own, ref) in enumerate(((own1, w1), (own2, w2))):
        half = own.shape[1] // 2
        cut = pl.ds(pl.multiple_of(other * half, 128), half)
        mine = pl.ds(pl.multiple_of(core * half, 128), half)
        swaps.append(remote(own.at[:, cut], ref.at[core, x, y, :, cut], swap_send.at[n], swap_recv.at[n], section=other))
        swaps[-1].start()
        locals_.append(pltpu.make_async_copy(own.at[:, mine], ref.at[core, x, y, :, mine], local.at[n]))
        locals_[-1].start()
    for n, ref in enumerate((w1, w2)):
        half = ref.shape[-1] // 2
        dst = ref.at[other, x, y, :, pl.ds(pl.multiple_of(core * half, 128), half)]
        locals_[n].wait()
        remote(dst, dst, swap_send.at[n], swap_recv.at[n], section=core).wait_recv()
        if n == 0:
            gathers[0][0].start()
    gathers[0][0].middle()
    gathers[0][1].start()
    complete(0, 0)
    keys = [
        PlaneGather(st["kv"].at[layer], pl.ds(0, 256), pl.ds(256, 256), kv_send.at[layer], kv_recv.at[layer])
        for layer in range(2)
    ]

    def mid_keys_first():
        gathers[0][1].middle()

    def mid_out_first():
        complete(0, 1)
        gathers[1][0].start()

    def mid_mlp_first():
        gathers[1][0].middle()
        gathers[1][1].start()

    def mid_keys_second():
        complete(1, 1)

    hidden = inputs.at[core]
    tables = first[...], cos[...], sin[...]
    sent = forward_layer(0, hidden, w1, w2, *tables, st, tp_sems, keys[0], mid_keys_first, mid_out_first, mid_mlp_first)
    gathers[1][1].middle()
    complete(1, 0)
    hidden = st["outs"].at[0]
    sent += forward_layer(1, hidden, w1, w2, *tables, st, tp_sems, keys[1], mid_keys_second, lambda: None, lambda: None)
    swaps.append(remote(st["outs"].at[other], outs_other, swap_send.at[2], swap_recv.at[2], section=other))
    swaps[-1].start()
    swaps[-1].wait_recv()
    finish(sent + swaps)
    for part in keys + gathers[0] + gathers[1]:
        part.finish()
    for copy in kept:
        copy.wait()


def run_forward(own1, own2, inputs, first, cos, sin):
    outs = KEPT + [((ROWS, WIDTH), BF)] + list(STASH.values())
    return pl.pallas_call(
        forward_kernel,
        out_shape=[jax.ShapeDtypeStruct(*o) for o in outs],
        in_specs=[VM] * 6,
        out_specs=[HB] * 4 + [VM] * len(STASH),
        scratch_shapes=[
            *[pltpu.VMEM(*k) for k in KEPT],
            pltpu.VMEM((4, ROWS, WIDTH), BF),
            pltpu.VMEM((4, TP - 1, SUB, WIDTH), BF),
            *[DMA((4, TP - 1))] * 4,
            DMA((2,)), DMA((3,)), DMA((3,)),
            DMA((4, 12)), DMA((4, 12)), DMA((4, 8)), DMA((4, 8)), DMA((2, 12)), DMA((2, 12)), DMA((2, 3)),
        ],
        compiler_params=params(1, 60),
    )(own1, own2, inputs, first, cos, sin)


def tp_rows(ref, index):
    return ref.at[pl.ds(pl.multiple_of(index * SUB, SUB), SUB)]


def tp_scatter_sum(part, landing, send, recv):
    here = lax.axis_index("tp")
    copies = []
    for step in range(1, TP):
        peer = ring("tp", step, TP)
        copies.append(
            remote(tp_rows(part, peer), landing.at[step - 1], send.at[step - 1], recv.at[step - 1], tp=peer)
        )
        copies[-1].start()
    total = tp_rows(part, here)[...].astype(F32)
    for step, copy in enumerate(copies):
        copy.wait_recv()
        total = total + landing[step].astype(F32)
    return total, copies


def tp_gather(full, send, recv):
    here = lax.axis_index("tp")
    copies = []
    for step in range(1, TP):
        peer = ring("tp", step, TP)
        place = tp_rows(full, here)
        copies.append(remote(place, place, send.at[step - 1], recv.at[step - 1], tp=peer))
        copies[-1].start()
    for step, copy in enumerate(copies):
        place = tp_rows(full, ring("tp", TP - 1 - step, TP))
        remote(place, place, send.at[step], recv.at[step], tp=here).wait_recv()
    return copies


def finish(copies):
    for copy in copies:
        copy.wait_send()


def norm_back(values, grad, gain):
    inverse = lax.rsqrt(jnp.mean(values * values, -1, keepdims=True) + EPSILON)
    unit = values * inverse
    scaled = grad * gain
    back = inverse * (scaled - unit * jnp.mean(scaled * unit, -1, keepdims=True))
    return back, jnp.sum(grad * unit, 0, keepdims=True)


class PlaneScatter:
    def __init__(self, ref, cols_a, cols_b, lands, send, recv):
        self.ref, self.a, self.b, self.send, self.recv = ref, cols_a, cols_b, send, recv
        self.lands = lands
        self.sent = []

    def push(self, src, land, slot, peer):
        copy = remote(src, land, self.send.at[slot], self.recv.at[slot], ctx=peer)
        copy.start()
        self.sent.append(copy)

    def add(self, own, phase, slot):
        land = self.lands[phase]
        for step in range(EDGE - 1):
            dst = land.at[step]
            sems = self.send.at[slot + step], self.recv.at[slot + step]
            remote(dst, dst, *sems, ctx=lax.axis_index("ctx")).wait_recv()
        total = own[...].astype(F32)
        for step in range(EDGE - 1):
            total = total + land[step].astype(F32)
        return total

    def start(self):
        x, y = place()
        for step in range(1, EDGE):
            self.push(self.ref.at[around(x, step), :, :, self.a], self.lands[0].at[step - 1], step - 1, peer_x(step))
            self.push(self.ref.at[:, around(y, step), :, self.b], self.lands[1].at[step - 1], step + 2, peer_y(step))

    def middle(self):
        x, y = place()
        own = self.ref.at[x, :, :, self.a]
        own[...] = self.add(own, 0, 0).astype(BF)
        for step in range(1, EDGE):
            self.push(self.ref.at[x, around(y, step), :, self.a], self.lands[2].at[step - 1], step + 5, peer_y(step))
        own = self.ref.at[:, y, :, self.b]
        own[...] = self.add(own, 1, 3).astype(BF)
        for step in range(1, EDGE):
            self.push(self.ref.at[around(x, step), y, :, self.b], self.lands[3].at[step - 1], step + 8, peer_x(step))

    def end(self):
        x, y = place()
        return self.add(self.ref.at[x, y, :, self.a], 2, 6), self.add(self.ref.at[x, y, :, self.b], 3, 9)

    def finish(self):
        finish(self.sent)


GRAD_HALF = {1024: (256, 256), REST: (768, 640)}


def scatter_lands(rows, first, second):
    return [
        ((EDGE - 1, EDGE, rows, first), BF),
        ((EDGE - 1, EDGE, rows, second), BF),
        ((EDGE - 1, rows, first), BF),
        ((EDGE - 1, rows, second), BF),
    ]


class GradScatter(PlaneScatter):
    def __init__(self, ref, lands, send, recv, pair_land, pair_send, pair_recv):
        half = ref.shape[-1] // 2
        first, second = GRAD_HALF[ref.shape[-1]]
        core = lax.axis_index("section")
        low = pl.multiple_of(core * half, 128)
        super().__init__(ref, pl.ds(low, first), pl.ds(pl.multiple_of(low + first, 128), second), lands, send, recv)
        self.mine = pl.ds(low, half)
        self.theirs = pl.ds(pl.multiple_of((1 - core) * half, 128), half)
        self.pair_land = pair_land
        self.pair = remote(ref.at[:, :, :, self.theirs], pair_land, pair_send, pair_recv, section=1 - core)
        self.half, self.first = half, first

    def swap(self):
        self.pair.start()

    def start(self):
        self.pair.wait_recv()
        for row in range(EDGE):
            own = self.ref.at[row, :, :, self.mine]
            own[...] = (own[...].astype(F32) + self.pair_land[row].astype(F32)).astype(BF)
        super().start()

    def finish(self):
        self.pair.wait_send()
        super().finish()

    def result(self, out):
        a, b = self.end()
        out[:, self.a] = a
        out[:, self.b] = b


def weight_grad(ref, low, left_t, right):
    size = right.shape[1]
    for row in range(EDGE):
        block = mm(left_t[row * 256 : (row + 1) * 256], right)
        ref[row, :, :, low : low + size] = block.reshape(EDGE, BLOCK, size).astype(BF)


def turn_back(grads, values, gain, cos, sin):
    outs, terms = [], 0.0
    for index in range(values.shape[1] // HEAD_SIZE):
        grad = head(grads, index)
        grad = grad * cos + pltpu.roll(grad * sin, HEAD_SIZE // 2, 1)
        back, term = norm_back(head(values, index), grad, gain)
        outs.append(back.astype(BF))
        terms = terms + term
    return jnp.concatenate(outs, 1), terms


def wide(buf, low, size):
    return buf[:, :, :, low : low + size].reshape(-1, size)


def tp_scatter(part, landing, send, recv):
    copies = []
    for step in range(1, TP):
        peer = ring("tp", step, TP)
        copies.append(
            remote(tp_rows(part, peer), landing.at[step - 1], send.at[step - 1], recv.at[step - 1], tp=peer)
        )
        copies[-1].start()
    return copies


def tp_total(part, landing, copies):
    total = tp_rows(part, lax.axis_index("tp"))[...].astype(F32)
    for step, copy in enumerate(copies):
        copy.wait_recv()
        total = total + landing[step].astype(F32)
    return total


def tp_spread(full, send, recv):
    here = lax.axis_index("tp")
    copies = []
    for step in range(1, TP):
        rows = tp_rows(full, here)
        copies.append(remote(rows, rows, send.at[step - 1], recv.at[step - 1], tp=ring("tp", step, TP)))
        copies[-1].start()
    return copies


def tp_spread_wait(full, send, recv):
    here = lax.axis_index("tp")
    for step in range(TP - 1):
        rows = tp_rows(full, ring("tp", TP - 1 - step, TP))
        remote(rows, rows, send.at[step], recv.at[step], tp=here).wait_recv()


BACK_IN = ("first", "cos", "sin", "inputs", "cotangent")
BACK_KEPT = [k[0][1:] for k in KEPT]
SMALL = (8, WIDTH)
LANDS = [
    *scatter_lands(BLOCK, *GRAD_HALF[REST]), *scatter_lands(BLOCK, *GRAD_HALF[1024]), *scatter_lands(ROWS, 256, 256)
]


def backward_kernel(w1_all, w2_all, kv_all, *refs):
    names = (*BACK_IN, *STASH)
    st = dict(zip(names, refs))
    inner, inner_other, g1_out, g2_out, small_out, *refs = refs[len(names) :]
    w1, w2, kv, dkv, g1, g2, res1, res2, pair1, pair2, part, landing, middle_grad, small, small_land, *refs = refs
    lands = [refs[n * len(LANDS) : (n + 1) * len(LANDS)] for n in range(2)]
    refs = refs[2 * len(LANDS) :]
    tp_sems, (load, send, recv, pair_send, pair_recv, small_send, small_recv, end_send, end_recv) = refs[:4], refs[4:]
    core = lax.axis_index("section")
    other = 1 - core
    here = lax.axis_index("tp")
    x, y = place()
    cos, sin, first = st["cos"][...], st["sin"][...], st["first"][...]
    sent = []
    loads = [
        [pltpu.make_async_copy(src.at[layer], dst, load.at[layer, n])
         for n, (src, dst) in enumerate(((w1_all, w1), (w2_all, w2), (kv_all, kv)))]
        for layer in range(2)
    ]
    for n in (1, 2, 0):
        loads[1][n].start()
    greet_plane()
    rest = [
        GradScatter(g2, lands[layer][0:4], send.at[layer, 0], recv.at[layer, 0],
                    pair2.at[layer], pair_send.at[layer, 0], pair_recv.at[layer, 0])
        for layer in range(2)
    ]
    head_grads = [
        GradScatter(g1, lands[layer][4:8], send.at[layer, 1], recv.at[layer, 1],
                    pair1.at[layer], pair_send.at[layer, 1], pair_recv.at[layer, 1])
        for layer in range(2)
    ]
    keys = [
        PlaneScatter(dkv, pl.ds(0, 256), pl.ds(256, 256), lands[layer][8:12], send.at[layer, 2], recv.at[layer, 2])
        for layer in range(2)
    ]
    small[...] = jnp.zeros(SMALL, F32)
    rows = pl.ds(pl.multiple_of(here * SUB, SUB), SUB)
    out_grad = st["cotangent"].at[core]
    for layer in (1, 0):
        hidden = st["outs"].at[0] if layer else st["inputs"].at[core]
        gains, head_gains = st["gains"][layer], st["head_gains"][layer]
        sems = [[s.at[2 * layer + n] for s in tp_sems] for n in range(2)]
        grad_low = out_grad[...]
        grad_rows = out_grad[rows, :].astype(F32)
        gate, up = st["gate"][layer], st["up"][layer]
        sigmoid = 1.0 / (1.0 + jnp.exp(-gate))
        loads[layer][1].wait()
        act_grad = mm(grad_low, wide(w2, DOWN, 768))
        gate_low = (act_grad * up * sigmoid * (1.0 + gate * (1.0 - sigmoid))).astype(BF)
        up_low = (act_grad * gate * sigmoid).astype(BF)
        activated = (gate * sigmoid * up).astype(BF)
        part[2 * layer] = (
            mm(gate_low, wide(w2, GATE, 768), (1, 1)) + mm(up_low, wide(w2, UP, 768), (1, 1))
        ).astype(BF)
        copies = tp_scatter(part.at[2 * layer], landing.at[2 * layer], *sems[0][:2])
        if layer == 0:
            rest[1].result(res2.at[1])
            rest[1].finish()
        mlp_t = st["mlp_in"][layer].T
        weight_grad(g2, GATE, mlp_t, gate_low)
        weight_grad(g2, UP, mlp_t, up_low)
        total = tp_total(part.at[2 * layer], landing.at[2 * layer], copies)
        sent += copies
        back, terms = norm_back(st["after"][layer], total, gains[1:2])
        small[3 * layer + 1 : 3 * layer + 2, :] = terms
        grad_rows = grad_rows + back
        full = middle_grad.at[layer]
        tp_rows(full, here)[...] = grad_rows.astype(BF)
        sent += tp_spread(full, *sems[0][2:])
        weight_grad(g2, DOWN, grad_low.T, activated)
        if layer == 0:
            head_grads[1].start()
        tp_spread_wait(full, *sems[0][2:])
        grad_low = full[...]
        mixed_grad = mm(grad_low, wide(w2, OUT, 512)).astype(BF)
        if layer == 1:
            loads[0][1].start()
        weight_grad(g2, OUT, grad_low.T, st["mixed"][layer])
        rest[layer].swap()
        loads[layer][2].wait()
        query = st["query"][layer]
        query_grads = []
        for group in range(2):
            group_keys = wide(kv, group * HEAD_SIZE, HEAD_SIZE)
            group_values = wide(kv, 256 + group * HEAD_SIZE, HEAD_SIZE)
            keys_t = group_keys.T
            key_grad, value_grad = 0.0, 0.0
            for index in (2 * group, 2 * group + 1):
                head_query, head_grad = head(query, index), head(mixed_grad, index)
                scores = scores_t(group_keys, head_query, first)
                prob = jnp.exp(scores - st["level"][layer, index : index + 1, :])
                prob_grad = mm(group_values, head_grad, (1, 1))
                dots = jnp.sum(prob * prob_grad, 0, keepdims=True)
                score_low = (prob * (prob_grad - dots)).astype(BF)
                query_grads.append(mm(keys_t, score_low).T * SCALE)
                key_grad = key_grad + mm(score_low, head_query)
                value_grad = value_grad + mm(prob.astype(BF), head_grad)
            shape = (EDGE, EDGE, ROWS, HEAD_SIZE)
            dkv[:, :, :, group * HEAD_SIZE : (group + 1) * HEAD_SIZE] = (key_grad * SCALE).astype(BF).reshape(shape)
            low = 256 + group * HEAD_SIZE
            dkv[:, :, :, low : low + HEAD_SIZE] = value_grad.astype(BF).reshape(shape)
        keys[layer].start()
        if layer == 1:
            loads[0][2].start()
        else:
            head_grads[1].middle()
        rest[layer].start()
        query_low, terms = turn_back(
            jnp.concatenate(query_grads, 1), st["query_proj"][layer], head_gains[0:1], cos, sin
        )
        small[3 * layer + 2 : 3 * layer + 3, 0:128] = terms
        normed_t = st["normed"][layer].T
        keys[layer].middle()
        if layer == 0:
            head_grads[1].result(res1.at[1])
            head_grads[1].finish()
        weight_grad(g1, 0, normed_t, query_low)
        key_grad, value_grad = keys[layer].end()
        keys[layer].finish()
        key_low, terms = turn_back(key_grad, st["key_proj"][layer], head_gains[1:2], cos, sin)
        small[3 * layer + 2 : 3 * layer + 3, 128:256] = terms
        joined = jnp.concatenate([query_low, key_low, value_grad.astype(BF)], 1)
        loads[layer][0].wait()
        part[2 * layer + 1] = mm(joined, wide(w1, 0, 1024), (1, 1)).astype(BF)
        if layer == 1:
            loads[0][0].start()
        copies = tp_scatter(part.at[2 * layer + 1], landing.at[2 * layer + 1], *sems[1][:2])
        weight_grad(g1, 512, normed_t, joined[:, 512:])
        head_grads[layer].swap()
        total = tp_total(part.at[2 * layer + 1], landing.at[2 * layer + 1], copies)
        sent += copies
        back, terms = norm_back(hidden[rows, :].astype(F32), total, gains[0:1])
        small[3 * layer : 3 * layer + 1, :] = terms
        full = inner.at[layer]
        tp_rows(full, here)[...] = (grad_rows + back).astype(BF)
        sent += tp_spread(full, *sems[1][2:])
        if layer == 0:
            head_grads[0].start()
        rest[layer].middle()
        tp_spread_wait(full, *sems[1][2:])
        out_grad = full
    ends = [remote(inner.at[other], inner_other, end_send.at[0], end_recv.at[0], section=other)]
    ends[0].start()

    def small_round(slot, peers):
        copies = []
        for n, where in enumerate(peers):
            copies.append(
                remote(small, small_land.at[slot + n], small_send.at[slot + n], small_recv.at[slot + n], **where)
            )
            copies[-1].start()
        return copies

    def small_add(slot, copies):
        for copy in copies:
            copy.wait()
        small[...] += sum(small_land[slot + n] for n in range(len(copies)))

    steps = range(1, EDGE)
    around_pair = small_round(0, [dict(section=other)])
    rest[0].result(res2.at[0])
    small_add(0, around_pair)
    around_x = small_round(1, [dict(ctx=peer_x(step)) for step in steps])
    head_grads[0].middle()
    small_add(1, around_x)
    around_y = small_round(4, [dict(ctx=peer_y(step)) for step in steps])
    head_grads[0].result(res1.at[0])
    mine = [head_grads[0].mine, rest[0].mine]
    for n, (res, out) in enumerate(((res1, g1_out), (res2, g2_out))):
        part_out = res.at[other, :, mine[n]]
        ends.append(remote(part_out, out.at[:, mine[n]], end_send.at[n + 1], end_recv.at[n + 1], section=other))
        ends[-1].start()
        out[:, mine[n]] = res[core, :, mine[n]]
    small_add(4, around_y)
    around_z = small_round(7, [dict(tp=ring("tp", step, TP)) for step in steps])
    small_add(7, around_z)
    small_out[...] = small[...]
    ends[0].wait_recv()
    for n, (grad, out) in enumerate(((head_grads[0], g1_out), (rest[0], g2_out))):
        dst = out.at[:, grad.theirs]
        remote(dst, dst, end_send.at[n + 1], end_recv.at[n + 1], section=core).wait_recv()
    finish(ends + sent)
    rest[0].finish()
    head_grads[0].finish()


def run_backward(w1, w2, kv, *args):
    outs = [
        ((2, ROWS, WIDTH), BF), ((ROWS, WIDTH), BF), ((BLOCK, 1024), F32), ((BLOCK, REST), F32), (SMALL, F32),
    ]
    return pl.pallas_call(
        backward_kernel,
        out_shape=[jax.ShapeDtypeStruct(*o) for o in outs],
        in_specs=[HB] * 3 + [VM] * len(args),
        out_specs=[VM, HB, VM, VM, VM],
        scratch_shapes=[
            *[pltpu.VMEM(k, BF) for k in BACK_KEPT],
            pltpu.VMEM((EDGE, EDGE, ROWS, 512), BF),
            pltpu.VMEM((EDGE, EDGE, BLOCK, 1024), BF),
            pltpu.VMEM((EDGE, EDGE, BLOCK, REST), BF),
            pltpu.VMEM((2, BLOCK, 1024), F32),
            pltpu.VMEM((2, BLOCK, REST), F32),
            pltpu.VMEM((2, EDGE, EDGE, BLOCK, 512), BF),
            pltpu.VMEM((2, EDGE, EDGE, BLOCK, REST // 2), BF),
            pltpu.VMEM((4, ROWS, WIDTH), BF),
            pltpu.VMEM((4, TP - 1, SUB, WIDTH), BF),
            pltpu.VMEM((2, ROWS, WIDTH), BF),
            pltpu.VMEM(SMALL, F32),
            pltpu.VMEM((10, *SMALL), F32),
            *[pltpu.VMEM(*k) for k in LANDS * 2],
            *[DMA((4, TP - 1))] * 4,
            DMA((2, 3)), DMA((2, 3, 12)), DMA((2, 3, 12)), DMA((2, 2)), DMA((2, 2)),
            DMA((10,)), DMA((10,)), DMA((3,)), DMA((3,)),
        ],
        compiler_params=params(2, 60),
    )(w1, w2, kv, *args)


def rotary(positions):
    half_dim = HEAD_SIZE // 2
    inv_freq = ROPE_BASE ** (-(jnp.arange(half_dim, dtype=F32) * 2.0 / HEAD_SIZE))
    angles = positions.astype(F32)[:, None] * inv_freq[None, :]
    return (jnp.cos(angles), jnp.sin(angles))


def wide_tables(token_pos):
    cos, sin = rotary(token_pos)
    return jnp.concatenate([cos, cos], 1), jnp.concatenate([-sin, sin], 1)


def on_device(
    inputs, positions, cotangent, attn_gain, w_query, w_key, w_value, query_gain, key_gain, w_output,
    mlp_gain, w_gate, w_up, w_down,
):
    core = lax.axis_index("section")
    token_pos = lax.dynamic_index_in_dim(positions, core, 0, keepdims=False)
    gains = jnp.concatenate([attn_gain.T, mlp_gain.T, jnp.zeros((BLOCK, 126), BF)], 1)
    heads = jnp.concatenate([query_gain, key_gain, jnp.zeros((BLOCK - 2, 128), BF)], 0)
    own1 = jnp.concatenate([w_query[0], w_key[0], w_value[0], gains, heads], 1)
    own2 = jnp.concatenate([w_gate[0], w_up[0], w_output[0].T, w_down[0].T], 1)
    first = (lax.axis_index("ctx") * ROWS + jnp.arange(ROWS, dtype=jnp.int32) - token_pos)[None]
    cos, sin = wide_tables(token_pos)
    w1, w2, kv, outs_other, *stash = run_forward(own1, own2, inputs, first, cos, sin)
    inner, inner_other, g1, g2, small = run_backward(w1, w2, kv, first, cos, sin, inputs, cotangent, *stash)
    outs = dict(zip(STASH, stash))["outs"]

    def both_micros(stacked, received):
        own = lax.dynamic_index_in_dim(stacked, core, 0, keepdims=False)
        low, high = jnp.where(core == 0, own, received), jnp.where(core == 0, received, own)
        return jnp.stack([low, high])[None]

    small = lax.dynamic_slice_in_dim(small, 3 * core, 3, 0)
    vectors = lax.dynamic_slice_in_dim(small[:2], lax.axis_index("ctx") * BLOCK, BLOCK, 1)
    return (
        both_micros(outs, outs_other),
        both_micros(inner, inner_other).astype(F32),
        vectors[0:1],
        g1[None, :, 0:512],
        g1[None, :, 512:768],
        g1[None, :, 768:1024],
        small[2:3, 0:128],
        small[2:3, 128:256],
        g2[:, OUT : OUT + 512].T[None],
        vectors[1:2],
        g2[None, :, GATE : GATE + 768],
        g2[None, :, UP : UP + 768],
        g2[:, DOWN : DOWN + 768].T[None],
    )


def solution(mesh):
    row, col = P("section", "ctx", "tp"), P("section", "tp", "ctx")
    gain, head = P("section", "ctx"), P("section", None)
    tokens = P(None, "ctx", None)
    layered = P("section", None, "ctx", None)
    return jax.shard_map(
        on_device,
        mesh=mesh,
        in_specs=(tokens, P(None, "ctx"), tokens, gain, row, row, row, head, head, col, gain, row, row, col),
        out_specs=(layered, layered, gain, row, row, row, head, head, col, gain, row, row, col),
        check_vma=False,
    )
```

```python
import math

import jax
import jax.numpy as jnp
import numpy as np
from jax import lax
from jax.experimental import pallas as pl
from jax.experimental.pallas import tpu as pltpu
from jax.sharding import PartitionSpec as P

HEAD_SIZE = 128
EPSILON = 1e-06
ROPE_BASE = 1000000.0
MASKED = -1e30
MESH = pl.DeviceIdType.MESH
BF = jnp.bfloat16
F32 = jnp.float32
CTX = 16
TP = 4
ROWS = 128
SUB = ROWS // TP
WIDTH = 1024
BLOCK = WIDTH // CTX
SCALE = 1.0 / math.sqrt(HEAD_SIZE)


def ring(axis, step, count):
    return lax.rem(lax.axis_index(axis) + step, count)


def remote(src, dst, send, recv, **where):
    return pltpu.make_async_remote_copy(
        src_ref=src, dst_ref=dst, send_sem=send, recv_sem=recv, device_id=where, device_id_type=MESH
    )


def params(collective_id, vmem=48):
    return pltpu.CompilerParams(
        collective_id=collective_id, has_side_effects=True, vmem_limit_bytes=vmem * 2**20
    )


VM = pl.BlockSpec(memory_space=pltpu.VMEM)
HB = pl.BlockSpec(memory_space=pl.ANY)
DMA = pltpu.SemaphoreType.DMA


EDGE = 4
HEADS = 4
FIRST = 1280
REST = 2816
GATE, UP, DOWN, OUT = 0, 768, 1536, 2304
GROUPS = ((0, 0, 1280, 384), (1, 2304, 512, 128), (1, 0, 2304, 640))


def place():
    here = lax.axis_index("ctx")
    return here // EDGE, lax.rem(here, EDGE)


def around(value, step):
    return lax.rem(value + step, EDGE)


def peer_x(step):
    x, y = place()
    return around(x, step) * EDGE + y


def peer_y(step):
    x, y = place()
    return x * EDGE + around(y, step)


def greet_plane():
    sem = pltpu.get_barrier_semaphore()
    for step in range(1, EDGE):
        for where in ({"ctx": peer_x(step)}, {"ctx": peer_y(step)}, {"tp": ring("tp", step, TP)}):
            pl.semaphore_signal(sem, inc=1, device_id=where, device_id_type=MESH)
    pl.semaphore_signal(
        sem, inc=1, device_id={"section": 1 - lax.axis_index("section")}, device_id_type=MESH
    )
    pl.semaphore_wait(sem, 3 * (EDGE - 1) + 1)


class PlaneGather:
    def __init__(self, ref, cols_a, cols_b, send, recv):
        self.ref, self.a, self.b, self.send, self.recv = ref, cols_a, cols_b, send, recv
        self.sent = []

    def push(self, src, slot, peer):
        copy = remote(src, src, self.send.at[slot], self.recv.at[slot], ctx=peer)
        copy.start()
        self.sent.append(copy)

    def wait(self, dst, slot):
        remote(dst, dst, self.send.at[slot], self.recv.at[slot], ctx=lax.axis_index("ctx")).wait_recv()

    def start(self):
        x, y = place()
        for step in range(1, EDGE):
            self.push(self.ref.at[x, y, :, self.a], step - 1, peer_x(step))
            self.push(self.ref.at[x, y, :, self.b], step + 2, peer_y(step))

    def middle(self):
        x, y = place()
        for step in range(1, EDGE):
            self.wait(self.ref.at[around(x, EDGE - step), y, :, self.a], step - 1)
        for step in range(1, EDGE):
            self.push(self.ref.at[:, y, :, self.a], step + 5, peer_y(step))
        for step in range(1, EDGE):
            self.wait(self.ref.at[x, around(y, EDGE - step), :, self.b], step + 2)
        for step in range(1, EDGE):
            self.push(self.ref.at[x, :, :, self.b], step + 8, peer_x(step))

    def second(self):
        x, y = place()
        for step in range(1, EDGE):
            yield self.ref.at[:, around(y, EDGE - step), :, self.a], step + 5
            yield self.ref.at[around(x, EDGE - step), :, :, self.b], step + 8

    def end(self):
        for dst, slot in self.second():
            self.wait(dst, slot)

    def finish(self):
        finish(self.sent)


class KeyGather(PlaneGather):
    def start(self):
        x, y = place()
        for step in (1, 3, 2):
            self.push(self.ref.at[x, y, :, self.a], step - 1, peer_x(step))
            self.push(self.ref.at[x, y, :, self.b], step + 14, peer_y(step))
        for step in (1, 3, 2):
            self.push(self.ref.at[x, y, :, self.a], step + 2, peer_y(step))
            self.push(self.ref.at[x, y, :, self.b], step + 17, peer_x(step))

    def middle(self):
        x, y = place()
        for step in (1, 3, 2):
            block = self.ref.at[around(x, EDGE - step), y, :, self.a]
            self.wait(block, step - 1)
            for to in (1, 3, 2):
                self.push(block, 3 * step + to + 2, peer_y(to))
            block = self.ref.at[x, around(y, EDGE - step), :, self.b]
            self.wait(block, step + 14)
            for to in (1, 3, 2):
                self.push(block, 3 * step + to + 17, peer_x(to))

    def end(self):
        x, y = place()
        for to in (1, 3, 2):
            self.wait(self.ref.at[x, around(y, EDGE - to), :, self.a], to + 2)
            self.wait(self.ref.at[around(x, EDGE - to), y, :, self.b], to + 17)
        for step in (1, 3, 2):
            for to in (1, 3, 2):
                self.wait(self.ref.at[around(x, EDGE - step), around(y, EDGE - to), :, self.a], 3 * step + to + 2)
                self.wait(self.ref.at[around(x, EDGE - to), around(y, EDGE - step), :, self.b], 3 * step + to + 17)


class WeightGather(PlaneGather):
    def __init__(self, ref, low, width, first, send, recv, pair_send, pair_recv):
        half = width // 2

        def cols(core):
            start = pl.multiple_of(low + core * half, 128)
            return pl.ds(start, first), pl.ds(pl.multiple_of(start + first, 128), half - first)

        core = lax.axis_index("section")
        super().__init__(ref, *cols(core), send, recv)
        self.theirs = cols(1 - core)
        self.pair_send, self.pair_recv = pair_send, pair_recv

    def hand(self, src, slot):
        other = 1 - lax.axis_index("section")
        copy = remote(src, src, self.pair_send.at[slot], self.pair_recv.at[slot], section=other)
        copy.start()
        self.sent.append(copy)

    def taken(self, dst, slot):
        here = lax.axis_index("section")
        remote(dst, dst, self.pair_send.at[slot], self.pair_recv.at[slot], section=here).wait_recv()

    def middle(self):
        super().middle()
        x, y = place()
        self.hand(self.ref.at[:, y, :, self.a], 0)
        self.hand(self.ref.at[x, :, :, self.b], 1)

    def end(self):
        x, y = place()
        for n, (dst, slot) in enumerate(self.second()):
            self.wait(dst, slot)
            self.hand(dst, n + 2)
        a, b = self.theirs
        self.taken(self.ref.at[:, y, :, a], 0)
        self.taken(self.ref.at[x, :, :, b], 1)
        for step in range(1, EDGE):
            self.taken(self.ref.at[:, around(y, EDGE - step), :, a], 2 * step)
            self.taken(self.ref.at[around(x, EDGE - step), :, :, b], 2 * step + 1)


def mm(a, b, contract=(1, 0)):
    return lax.dot_general(a, b, (((contract[0],), (contract[1],)), ((), ())), preferred_element_type=F32)


def flat(ref, layer, low, size):
    value = ref[layer, :, :, :, low : low + size]
    return value.reshape(-1, size)


def unit_rms(values):
    return values * lax.rsqrt(jnp.mean(values * values, -1, keepdims=True) + EPSILON)


def head(value, index):
    return value[:, index * HEAD_SIZE : (index + 1) * HEAD_SIZE]


def turn(values, gain, cos, sin):
    outs = []
    for index in range(values.shape[1] // HEAD_SIZE):
        scaled = unit_rms(head(values, index)) * gain
        outs.append(scaled * cos + pltpu.roll(scaled, HEAD_SIZE // 2, 1) * sin)
    return jnp.concatenate(outs, 1).astype(BF)


def scores_t(keys, query, first):
    raw = mm(keys, query, (1, 1)) * SCALE
    rows = lax.broadcasted_iota(jnp.int32, raw.shape, 0)
    last = lax.axis_index("ctx") * ROWS + lax.broadcasted_iota(jnp.int32, (1, ROWS), 1)
    return jnp.where((rows <= last) & (rows >= first), raw, MASKED)


def forward_layer(layer, hidden, w1, w2, first, cos, sin, st, tp_sems, keys_gather, groups, following):
    here = lax.axis_index("tp")
    x, y = place()
    rows = pl.ds(pl.multiple_of(here * SUB, SUB), SUB)
    part, landing = st["part"], st["landing"]
    groups[0].end()
    gains = flat(w1, layer, 1024, 128).astype(F32).T[:8]
    st["gains"][layer] = gains
    heads = w1[layer, 0, 0, 0:16, 1152:1280].astype(F32)
    st["head_gains"][layer] = heads[:8]
    normed = (unit_rms(hidden[...].astype(F32)) * gains[0:1]).astype(BF)
    st["normed"][layer] = normed
    key_proj = mm(normed, flat(w1, layer, 512, 256))
    value = mm(normed, flat(w1, layer, 768, 256))
    st["key_proj"][layer] = key_proj
    kv = st["kv"]
    kv[layer, x, y, :, 0:256] = turn(key_proj, heads[1:2], cos, sin)
    kv[layer, x, y, :, 256:512] = value.astype(BF)
    keys_gather.start()
    query_proj = mm(normed, flat(w1, layer, 0, 512))
    st["query_proj"][layer] = query_proj
    query = turn(query_proj, heads[0:1], cos, sin)
    st["query"][layer] = query
    st["keep"](0, layer)
    keys_gather.middle()
    if following:
        groups[1].middle()
    keys_gather.end()
    st["keep"](2, layer)
    groups[2].middle()
    mixed = []
    for group in range(2):
        keys = flat(kv, layer, group * HEAD_SIZE, HEAD_SIZE)
        values_t = flat(kv, layer, 256 + group * HEAD_SIZE, HEAD_SIZE).T
        for index in (2 * group, 2 * group + 1):
            scores = scores_t(keys, head(query, index), first)
            top = jnp.max(scores, 0, keepdims=True)
            raised = jnp.exp(scores - top)
            total = jnp.sum(raised, 0, keepdims=True)
            low = (raised * (1.0 / total)).astype(BF)
            st["level"][layer, index : index + 1, :] = top + jnp.log(total)
            mixed.append(mm(values_t, low).T.astype(BF))
    mixed = jnp.concatenate(mixed, 1)
    st["mixed"][layer] = mixed
    groups[1].end()
    part[2 * layer] = mm(mixed, flat(w2, layer, OUT, 512), (1, 1)).astype(BF)
    sems = [s.at[2 * layer] for s in tp_sems]
    sent = tp_scatter(part.at[2 * layer], landing.at[2 * layer], sems[0], sems[1])
    if following:
        following[0].start()
    total = tp_total(part.at[2 * layer], landing.at[2 * layer], sent)
    after = total + hidden[rows, :].astype(F32)
    st["after"][layer] = after
    mlp_in = st["mlp_in"].at[layer]
    mlp_in[rows, :] = (unit_rms(after) * gains[1:2]).astype(BF)
    sent += tp_spread(mlp_in, sems[2], sems[3])
    if following:
        following[0].middle()
    groups[2].end()
    tp_spread_wait(mlp_in, sems[2], sems[3])
    gate = mm(mlp_in[...], flat(w2, layer, GATE, 768))
    up = mm(mlp_in[...], flat(w2, layer, UP, 768))
    st["gate"][layer] = gate
    st["up"][layer] = up
    activated = (gate / (1.0 + jnp.exp(-gate)) * up).astype(BF)
    st["keep"](1, layer)
    if following:
        for group in following[1:]:
            group.start()
    part[2 * layer + 1] = mm(activated, flat(w2, layer, DOWN, 768), (1, 1)).astype(BF)
    sems = [s.at[2 * layer + 1] for s in tp_sems]
    copies = tp_scatter(part.at[2 * layer + 1], landing.at[2 * layer + 1], sems[0], sems[1])
    total = tp_total(part.at[2 * layer + 1], landing.at[2 * layer + 1], copies)
    out = st["outs"].at[layer]
    out[rows, :] = (total + after).astype(BF)
    copies += tp_spread(out, sems[2], sems[3])
    if following:
        following[1].middle()
    tp_spread_wait(out, sems[2], sems[3])
    return sent + copies


STASH = dict(
    first=((1, ROWS), jnp.int32),
    cos=((ROWS, HEAD_SIZE), F32),
    sin=((ROWS, HEAD_SIZE), F32),
    normed=((2, ROWS, WIDTH), BF),
    query_proj=((2, ROWS, 512), F32),
    key_proj=((2, ROWS, 256), F32),
    query=((2, ROWS, 512), BF),
    level=((2, 8, ROWS), F32),
    mixed=((2, ROWS, 512), BF),
    after=((2, SUB, WIDTH), F32),
    mlp_in=((2, ROWS, WIDTH), BF),
    gate=((2, ROWS, 768), F32),
    up=((2, ROWS, 768), F32),
    outs=((2, ROWS, WIDTH), BF),
    gains=((2, 8, WIDTH), F32),
    head_gains=((2, 8, HEAD_SIZE), F32),
)
KEPT = [
    ((2, EDGE, EDGE, BLOCK, FIRST), BF),
    ((2, EDGE, EDGE, BLOCK, REST), BF),
    ((2, EDGE, EDGE, ROWS, 512), BF),
]


def forward_kernel(
    inputs, positions, attn_gain, w_query, w_key, w_value, query_gain, key_gain, w_output, mlp_gain, w_gate, w_up,
    w_down, speeds, w1_out, w2_out, kv_out, *refs
):
    st = dict(zip(STASH, refs))
    own1, own2, w1, w2, st["kv"], st["part"], st["landing"], *refs = refs[len(STASH) :]
    tp_sems, (local, swap_send, swap_recv, send, recv, pair_send, pair_recv, kv_send, kv_recv, keep) = refs[:4], refs[4:]
    core = lax.axis_index("section")
    other = 1 - core
    x, y = place()
    kept = []

    def keep_copy(n, layer):
        src, dst = ((w1, w1_out), (w2, w2_out), (st["kv"], kv_out))[n]
        kept.append(pltpu.make_async_copy(src.at[layer], dst.at[layer], keep.at[layer, n]))
        kept[-1].start()

    st["keep"] = keep_copy
    gathers = [
        [
            WeightGather((w1, w2)[which].at[layer], low, width, along_x, send.at[layer, n], recv.at[layer, n],
                         pair_send.at[layer, n], pair_recv.at[layer, n])
            for n, (which, low, width, along_x) in enumerate(GROUPS)
        ]
        for layer in range(2)
    ]
    own1[:, 0:512] = w_query[0]
    own1[:, 512:768] = w_key[0]
    own1[:, 768:1024] = w_value[0]
    tail = [attn_gain[...].astype(F32), mlp_gain[...].astype(F32), jnp.zeros((126, BLOCK), F32)]
    own1[:, 1024:1152] = jnp.concatenate(tail, 0).T.astype(BF)
    tail = [query_gain[...].astype(F32), key_gain[...].astype(F32), jnp.zeros((BLOCK - 2, HEAD_SIZE), F32)]
    own1[:, 1152:1280] = jnp.concatenate(tail, 0).astype(BF)
    own2[:, GATE : GATE + 768] = w_gate[0]
    own2[:, UP : UP + 768] = w_up[0]
    own2[:, OUT : OUT + 512] = w_output[0]
    own2[:, DOWN : DOWN + 768] = w_down[0]
    greet_plane()
    swaps, locals_ = [], []
    for n, (own, ref) in enumerate(((own1, w1), (own2, w2))):
        for low, width in [(g[1], g[2]) for g in GROUPS if g[0] == n]:
            slot = len(swaps)
            half = width // 2
            cut = pl.ds(pl.multiple_of(low + other * half, 128), half)
            mine = pl.ds(pl.multiple_of(low + core * half, 128), half)
            swaps.append(
                remote(own.at[:, cut], ref.at[core, x, y, :, cut], swap_send.at[slot], swap_recv.at[slot], section=other)
            )
            swaps[-1].start()
            locals_.append(pltpu.make_async_copy(own.at[:, mine], ref.at[core, x, y, :, mine], local.at[slot]))
            locals_[-1].start()
    for slot, (n, low, width, _) in enumerate(GROUPS):
        half = width // 2
        dst = (w1, w2)[n].at[other, x, y, :, pl.ds(pl.multiple_of(low + core * half, 128), half)]
        locals_[slot].wait()
        remote(dst, dst, swap_send.at[slot], swap_recv.at[slot], section=core).wait_recv()
        if slot == 0:
            gathers[0][0].start()
    gathers[0][0].middle()
    for group in gathers[0][1:]:
        group.start()
    keys = [
        KeyGather(st["kv"].at[layer], pl.ds(0, 256), pl.ds(256, 256), kv_send.at[layer], kv_recv.at[layer])
        for layer in range(2)
    ]
    token_pos = positions[pl.ds(core, 1), :]
    first = lax.axis_index("ctx") * ROWS + lax.broadcasted_iota(jnp.int32, (1, ROWS), 1) - token_pos
    angles = jnp.broadcast_to(token_pos.astype(F32), (ROWS, ROWS)).T * speeds[...]
    cos, sin = jnp.cos(angles), jnp.sin(angles)
    low_half = lax.broadcasted_iota(jnp.int32, (ROWS, HEAD_SIZE), 1) < HEAD_SIZE // 2
    tables = first, cos, jnp.where(low_half, -sin, sin)
    for name, table in zip(("first", "cos", "sin"), tables):
        st[name][...] = table
    sent = forward_layer(0, inputs.at[core], w1, w2, *tables, st, tp_sems, keys[0], gathers[0], gathers[1])
    sent += forward_layer(1, st["outs"].at[0], w1, w2, *tables, st, tp_sems, keys[1], gathers[1], None)
    finish(sent + swaps)
    for part in keys + gathers[0] + gathers[1]:
        part.finish()
    for copy in kept:
        copy.wait()


def run_forward(*args):
    outs = KEPT + list(STASH.values())
    speeds = ROPE_BASE ** (-(np.arange(HEAD_SIZE // 2, dtype=np.float32) * np.float32(2.0 / HEAD_SIZE)))
    speeds = jnp.asarray(np.tile(speeds, 2)[None].astype(np.float32))
    return pl.pallas_call(
        forward_kernel,
        out_shape=[jax.ShapeDtypeStruct(*o) for o in outs],
        in_specs=[VM] * (len(args) + 1),
        out_specs=[HB] * 3 + [VM] * len(STASH),
        scratch_shapes=[
            pltpu.VMEM((BLOCK, FIRST), BF),
            pltpu.VMEM((BLOCK, REST), BF),
            *[pltpu.VMEM(*k) for k in KEPT],
            pltpu.VMEM((4, ROWS, WIDTH), BF),
            pltpu.VMEM((4, TP - 1, SUB, WIDTH), BF),
            *[DMA((4, TP - 1))] * 4,
            DMA((3,)), DMA((3,)), DMA((3,)),
            DMA((2, 3, 12)), DMA((2, 3, 12)), DMA((2, 3, 8)), DMA((2, 3, 8)), DMA((2, 30)), DMA((2, 30)), DMA((2, 3)),
        ],
        compiler_params=params(1, 60),
    )(*args, speeds)


def tp_rows(ref, index):
    return ref.at[pl.ds(pl.multiple_of(index * SUB, SUB), SUB)]


def tp_scatter(part, landing, send, recv):
    copies = []
    for step in range(1, TP):
        peer = ring("tp", step, TP)
        copies.append(
            remote(tp_rows(part, peer), landing.at[step - 1], send.at[step - 1], recv.at[step - 1], tp=peer)
        )
        copies[-1].start()
    return copies


def tp_total(part, landing, copies):
    total = tp_rows(part, lax.axis_index("tp"))[...].astype(F32)
    for step, copy in enumerate(copies):
        copy.wait_recv()
        total = total + landing[step].astype(F32)
    return total


def tp_spread(full, send, recv):
    here = lax.axis_index("tp")
    copies = []
    for step in range(1, TP):
        rows = tp_rows(full, here)
        copies.append(remote(rows, rows, send.at[step - 1], recv.at[step - 1], tp=ring("tp", step, TP)))
        copies[-1].start()
    return copies


def tp_spread_wait(full, send, recv):
    here = lax.axis_index("tp")
    for step in range(TP - 1):
        rows = tp_rows(full, ring("tp", TP - 1 - step, TP))
        remote(rows, rows, send.at[step], recv.at[step], tp=here).wait_recv()


def finish(copies):
    for copy in copies:
        copy.wait_send()


def norm_back(values, grad, gain):
    inverse = lax.rsqrt(jnp.mean(values * values, -1, keepdims=True) + EPSILON)
    unit = values * inverse
    scaled = grad * gain
    back = inverse * (scaled - unit * jnp.mean(scaled * unit, -1, keepdims=True))
    return back, jnp.sum(grad * unit, 0, keepdims=True)


class PlaneScatter:
    def __init__(self, ref, cols_a, cols_b, lands, send, recv):
        self.ref, self.a, self.b, self.send, self.recv = ref, cols_a, cols_b, send, recv
        self.lands = lands
        self.sent = []

    def push(self, src, land, slot, peer):
        copy = remote(src, land, self.send.at[slot], self.recv.at[slot], ctx=peer)
        copy.start()
        self.sent.append(copy)

    def add(self, own, phase, slot):
        land = self.lands[phase]
        for step in range(EDGE - 1):
            dst = land.at[step]
            sems = self.send.at[slot + step], self.recv.at[slot + step]
            remote(dst, dst, *sems, ctx=lax.axis_index("ctx")).wait_recv()
        total = own[...].astype(F32)
        for step in range(EDGE - 1):
            total = total + land[step].astype(F32)
        return total

    def start(self):
        x, y = place()
        for step in range(1, EDGE):
            self.push(self.ref.at[around(x, step), :, :, self.a], self.lands[0].at[step - 1], step - 1, peer_x(step))
            self.push(self.ref.at[:, around(y, step), :, self.b], self.lands[1].at[step - 1], step + 2, peer_y(step))

    def middle(self):
        x, y = place()
        own = self.ref.at[x, :, :, self.a]
        own[...] = self.add(own, 0, 0).astype(BF)
        for step in range(1, EDGE):
            self.push(self.ref.at[x, around(y, step), :, self.a], self.lands[2].at[step - 1], step + 5, peer_y(step))
        own = self.ref.at[:, y, :, self.b]
        own[...] = self.add(own, 1, 3).astype(BF)
        for step in range(1, EDGE):
            self.push(self.ref.at[around(x, step), y, :, self.b], self.lands[3].at[step - 1], step + 8, peer_x(step))

    def end(self):
        x, y = place()
        return self.add(self.ref.at[x, y, :, self.a], 2, 6), self.add(self.ref.at[x, y, :, self.b], 3, 9)

    def finish(self):
        finish(self.sent)


GRAD_HALF = {1024: (256, 256), REST: (768, 640)}


def scatter_lands(rows, first, second):
    return [
        ((EDGE - 1, EDGE, rows, first), BF),
        ((EDGE - 1, EDGE, rows, second), BF),
        ((EDGE - 1, rows, first), BF),
        ((EDGE - 1, rows, second), BF),
    ]


class GradScatter(PlaneScatter):
    def __init__(self, ref, lands, send, recv, pair_land, pair_send, pair_recv):
        half = ref.shape[-1] // 2
        first, second = GRAD_HALF[ref.shape[-1]]
        core = lax.axis_index("section")
        low = pl.multiple_of(core * half, 128)
        super().__init__(ref, pl.ds(low, first), pl.ds(pl.multiple_of(low + first, 128), second), lands, send, recv)
        self.mine = pl.ds(low, half)
        self.theirs = pl.ds(pl.multiple_of((1 - core) * half, 128), half)
        self.pair_land = pair_land
        self.pair = remote(ref.at[:, :, :, self.theirs], pair_land, pair_send, pair_recv, section=1 - core)
        self.half, self.first = half, first

    def swap(self):
        self.pair.start()

    def start(self):
        self.pair.wait_recv()
        for row in range(EDGE):
            own = self.ref.at[row, :, :, self.mine]
            own[...] = (own[...].astype(F32) + self.pair_land[row].astype(F32)).astype(BF)
        super().start()

    def finish(self):
        self.pair.wait_send()
        super().finish()

    def result(self, out):
        a, b = self.end()
        out[:, self.a] = a
        out[:, self.b] = b


def weight_grad(ref, low, left_t, right):
    size = right.shape[1]
    for row in range(EDGE):
        block = mm(left_t[row * 256 : (row + 1) * 256], right)
        ref[row, :, :, low : low + size] = block.reshape(EDGE, BLOCK, size).astype(BF)


def turn_back(grads, values, gain, cos, sin):
    outs, terms = [], 0.0
    for index in range(values.shape[1] // HEAD_SIZE):
        grad = head(grads, index)
        grad = grad * cos + pltpu.roll(grad * sin, HEAD_SIZE // 2, 1)
        back, term = norm_back(head(values, index), grad, gain)
        outs.append(back.astype(BF))
        terms = terms + term
    return jnp.concatenate(outs, 1), terms


def wide(buf, low, size):
    return buf[:, :, :, low : low + size].reshape(-1, size)


BACK_IN = ("inputs", "cotangent")
BACK_KEPT = [(EDGE, EDGE, BLOCK, 1024), *[k[0][1:] for k in KEPT[1:]]]
SMALL = (8, WIDTH)
LANDS = [
    *scatter_lands(BLOCK, *GRAD_HALF[REST]), *scatter_lands(BLOCK, *GRAD_HALF[1024]), *scatter_lands(ROWS, 256, 256)
]


def backward_kernel(w1_all, w2_all, kv_all, *refs):
    names = (*BACK_IN, *STASH)
    st = dict(zip(names, refs))
    inner, inner_other, outs_other, g1_out, g2_out, small_out, *refs = refs[len(names) :]
    w1, w2, kv, dkv, g1, g2, res1, res2, pair1, pair2, part, landing, middle_grad, small, small_land, *refs = refs
    lands = [refs[n * len(LANDS) : (n + 1) * len(LANDS)] for n in range(2)]
    refs = refs[2 * len(LANDS) :]
    tp_sems, (load, send, recv, pair_send, pair_recv, small_send, small_recv, end_send, end_recv) = refs[:4], refs[4:]
    core = lax.axis_index("section")
    other = 1 - core
    here = lax.axis_index("tp")
    x, y = place()
    cos, sin, first = st["cos"][...], st["sin"][...], st["first"][...]
    sent = []
    loads = [
        [pltpu.make_async_copy(src, dst, load.at[layer, n])
         for n, (src, dst) in enumerate(
             ((w1_all.at[layer, :, :, :, 0:1024], w1), (w2_all.at[layer], w2), (kv_all.at[layer], kv)))]
        for layer in range(2)
    ]
    for n in (1, 2, 0):
        loads[1][n].start()
    greet_plane()
    rest = [
        GradScatter(g2.at[layer], lands[layer][0:4], send.at[layer, 0], recv.at[layer, 0],
                    pair2.at[layer], pair_send.at[layer, 0], pair_recv.at[layer, 0])
        for layer in range(2)
    ]
    head_grads = [
        GradScatter(g1, lands[layer][4:8], send.at[layer, 1], recv.at[layer, 1],
                    pair1.at[layer], pair_send.at[layer, 1], pair_recv.at[layer, 1])
        for layer in range(2)
    ]
    keys = [
        PlaneScatter(dkv, pl.ds(0, 256), pl.ds(256, 256), lands[layer][8:12], send.at[layer, 2], recv.at[layer, 2])
        for layer in range(2)
    ]
    small[...] = jnp.zeros(SMALL, F32)
    ends = [remote(st["outs"].at[other], outs_other, end_send.at[3], end_recv.at[3], section=other)]
    ends[0].start()
    rows = pl.ds(pl.multiple_of(here * SUB, SUB), SUB)
    def small_round(slot, peers):
        copies = []
        for n, where in enumerate(peers):
            copies.append(
                remote(small, small_land.at[slot + n], small_send.at[slot + n], small_recv.at[slot + n], **where)
            )
            copies[-1].start()
        return copies

    def small_add(slot, copies):
        for copy in copies:
            copy.wait()
        small[...] += sum(small_land[slot + n] for n in range(len(copies)))

    out_grad = st["cotangent"].at[core]
    for layer in (1, 0):
        hidden = st["outs"].at[0] if layer else st["inputs"].at[core]
        gains, head_gains = st["gains"][layer], st["head_gains"][layer]
        sems = [[s.at[2 * layer + n] for s in tp_sems] for n in range(2)]
        grad_low = out_grad[...]
        grad_rows = out_grad[rows, :].astype(F32)
        gate, up = st["gate"][layer], st["up"][layer]
        sigmoid = 1.0 / (1.0 + jnp.exp(-gate))
        loads[layer][1].wait()
        act_grad = mm(grad_low, wide(w2, DOWN, 768))
        gate_low = (act_grad * up * sigmoid * (1.0 + gate * (1.0 - sigmoid))).astype(BF)
        up_low = (act_grad * gate * sigmoid).astype(BF)
        activated = (gate * sigmoid * up).astype(BF)
        part[2 * layer] = (
            mm(gate_low, wide(w2, GATE, 768), (1, 1)) + mm(up_low, wide(w2, UP, 768), (1, 1))
        ).astype(BF)
        copies = tp_scatter(part.at[2 * layer], landing.at[2 * layer], *sems[0][:2])
        if layer == 0:
            rest[1].middle()
            head_grads[1].start()
        mlp_t = st["mlp_in"][layer].T
        weight_grad(g2.at[layer], GATE, mlp_t, gate_low)
        weight_grad(g2.at[layer], UP, mlp_t, up_low)
        total = tp_total(part.at[2 * layer], landing.at[2 * layer], copies)
        sent += copies
        back, terms = norm_back(st["after"][layer], total, gains[1:2])
        small[3 * layer + 1 : 3 * layer + 2, :] = terms
        grad_rows = grad_rows + back
        full = middle_grad.at[layer]
        tp_rows(full, here)[...] = grad_rows.astype(BF)
        sent += tp_spread(full, *sems[0][2:])
        weight_grad(g2.at[layer], DOWN, grad_low.T, activated)
        if layer == 0:
            rest[1].result(res2.at[1])
        tp_spread_wait(full, *sems[0][2:])
        grad_low = full[...]
        mixed_grad = mm(grad_low, wide(w2, OUT, 512)).astype(BF)
        if layer == 1:
            loads[0][1].start()
        weight_grad(g2.at[layer], OUT, grad_low.T, st["mixed"][layer])
        rest[layer].swap()
        loads[layer][2].wait()
        query = st["query"][layer]
        query_grads = []
        if layer == 0:
            head_grads[1].middle()
        for group in range(2):
            group_keys = wide(kv, group * HEAD_SIZE, HEAD_SIZE)
            group_values = wide(kv, 256 + group * HEAD_SIZE, HEAD_SIZE)
            keys_t = group_keys.T
            key_grad, value_grad = 0.0, 0.0
            for index in (2 * group, 2 * group + 1):
                head_query, head_grad = head(query, index), head(mixed_grad, index)
                scores = scores_t(group_keys, head_query, first)
                prob = jnp.exp(scores - st["level"][layer, index : index + 1, :])
                prob_grad = mm(group_values, head_grad, (1, 1))
                dots = jnp.sum(prob * prob_grad, 0, keepdims=True)
                score_low = (prob * (prob_grad - dots)).astype(BF)
                query_grads.append(mm(keys_t, score_low).T * SCALE)
                key_grad = key_grad + mm(score_low, head_query)
                value_grad = value_grad + mm(prob.astype(BF), head_grad)
            shape = (EDGE, EDGE, ROWS, HEAD_SIZE)
            dkv[:, :, :, group * HEAD_SIZE : (group + 1) * HEAD_SIZE] = (key_grad * SCALE).astype(BF).reshape(shape)
            low = 256 + group * HEAD_SIZE
            dkv[:, :, :, low : low + HEAD_SIZE] = value_grad.astype(BF).reshape(shape)
        keys[layer].start()
        if layer == 1:
            loads[0][2].start()
        query_low, terms = turn_back(
            jnp.concatenate(query_grads, 1), st["query_proj"][layer], head_gains[0:1], cos, sin
        )
        small[3 * layer + 2 : 3 * layer + 3, 0:128] = terms
        normed_t = st["normed"][layer].T
        if layer == 0:
            head_grads[1].result(res1.at[1])
            head_grads[1].finish()
        keys[layer].middle()
        rest[layer].start()
        weight_grad(g1, 0, normed_t, query_low)
        key_grad, value_grad = keys[layer].end()
        keys[layer].finish()
        key_low, terms = turn_back(key_grad, st["key_proj"][layer], head_gains[1:2], cos, sin)
        small[3 * layer + 2 : 3 * layer + 3, 128:256] = terms
        joined = jnp.concatenate([query_low, key_low, value_grad.astype(BF)], 1)
        loads[layer][0].wait()
        part[2 * layer + 1] = mm(joined, wide(w1, 0, 1024), (1, 1)).astype(BF)
        if layer == 1:
            loads[0][0].start()
        copies = tp_scatter(part.at[2 * layer + 1], landing.at[2 * layer + 1], *sems[1][:2])
        weight_grad(g1, 512, normed_t, joined[:, 512:])
        head_grads[layer].swap()
        total = tp_total(part.at[2 * layer + 1], landing.at[2 * layer + 1], copies)
        sent += copies
        back, terms = norm_back(hidden[rows, :].astype(F32), total, gains[0:1])
        small[3 * layer : 3 * layer + 1, :] = terms
        full = inner.at[layer]
        tp_rows(full, here)[...] = (grad_rows + back).astype(BF)
        sent += tp_spread(full, *sems[1][2:])
        if layer == 0:
            around_pair = small_round(0, [dict(section=other)])
            rest[0].middle()
            head_grads[0].start()
        tp_spread_wait(full, *sems[1][2:])
        out_grad = full
    ends.append(remote(inner.at[other], inner_other, end_send.at[0], end_recv.at[0], section=other))
    ends[1].start()

    steps = range(1, EDGE)

    def deliver(n, grad, res, out):
        grad.result(res.at[0])
        part_out = res.at[other, :, grad.mine]
        ends.append(remote(part_out, out.at[:, grad.mine], end_send.at[n], end_recv.at[n], section=other))
        ends[-1].start()
        out[:, grad.mine] = res[core, :, grad.mine]

    small_add(0, around_pair)
    around_x = small_round(1, [dict(ctx=peer_x(step)) for step in steps])
    head_grads[0].middle()
    small_add(1, around_x)
    around_y = small_round(4, [dict(ctx=peer_y(step)) for step in steps])
    deliver(2, rest[0], res2, g2_out)
    small_add(4, around_y)
    around_z = small_round(7, [dict(tp=ring("tp", step, TP)) for step in steps])
    deliver(1, head_grads[0], res1, g1_out)
    small_add(7, around_z)
    small_out[...] = small[...]
    ends[0].wait_recv()
    ends[1].wait_recv()
    for n, grad, out in ((2, rest[0], g2_out), (1, head_grads[0], g1_out)):
        dst = out.at[:, grad.theirs]
        remote(dst, dst, end_send.at[n], end_recv.at[n], section=core).wait_recv()
    finish(ends + sent)
    for grad in (*rest, head_grads[0]):
        grad.finish()


def run_backward(w1, w2, kv, *args):
    outs = [
        ((2, ROWS, WIDTH), BF), ((ROWS, WIDTH), BF), ((ROWS, WIDTH), BF), ((BLOCK, 1024), F32), ((BLOCK, REST), F32), (SMALL, F32),
    ]
    return pl.pallas_call(
        backward_kernel,
        out_shape=[jax.ShapeDtypeStruct(*o) for o in outs],
        in_specs=[HB] * 3 + [VM] * len(args),
        out_specs=[VM, HB, HB, VM, VM, VM],
        scratch_shapes=[
            *[pltpu.VMEM(k, BF) for k in BACK_KEPT],
            pltpu.VMEM((EDGE, EDGE, ROWS, 512), BF),
            pltpu.VMEM((EDGE, EDGE, BLOCK, 1024), BF),
            pltpu.VMEM((2, EDGE, EDGE, BLOCK, REST), BF),
            pltpu.VMEM((2, BLOCK, 1024), F32),
            pltpu.VMEM((2, BLOCK, REST), F32),
            pltpu.VMEM((2, EDGE, EDGE, BLOCK, 512), BF),
            pltpu.VMEM((2, EDGE, EDGE, BLOCK, REST // 2), BF),
            pltpu.VMEM((4, ROWS, WIDTH), BF),
            pltpu.VMEM((4, TP - 1, SUB, WIDTH), BF),
            pltpu.VMEM((2, ROWS, WIDTH), BF),
            pltpu.VMEM(SMALL, F32),
            pltpu.VMEM((10, *SMALL), F32),
            *[pltpu.VMEM(*k) for k in LANDS * 2],
            *[DMA((4, TP - 1))] * 4,
            DMA((2, 3)), DMA((2, 3, 12)), DMA((2, 3, 12)), DMA((2, 2)), DMA((2, 2)),
            DMA((10,)), DMA((10,)), DMA((4,)), DMA((4,)),
        ],
        compiler_params=params(2, 62),
    )(w1, w2, kv, *args)


def results_kernel(
    outs_all, outs_other_all, inner_all, inner_other_all, g1_all, g2_all, small_all, section_out, input_grad,
    attn_gain, query, key, value, query_gain, key_gain, output, mlp_gain, gate, up, down, *refs
):
    core, here = lax.axis_index("section"), lax.axis_index("ctx")
    loads = [
        pltpu.make_async_copy(src, dst, refs[-1].at[n])
        for n, (src, dst) in enumerate(
            zip(
                (outs_all.at[core], outs_other_all, inner_all.at[core], inner_other_all, g1_all, g2_all, small_all),
                refs[:-1],
            )
        )
    ]
    for load in loads:
        load.start()
    outs, outs_other, inner, inner_other, g1, g2, small = refs[:-1]
    for load in loads:
        load.wait()
    section_out[0, core] = outs[...]
    section_out[0, 1 - core] = outs_other[...]
    input_grad[0, core] = inner[...].astype(F32)
    input_grad[0, 1 - core] = inner_other[...].astype(F32)
    query[0] = g1[:, 0:512]
    key[0] = g1[:, 512:768]
    value[0] = g1[:, 768:1024]
    gate[0] = g2[:, GATE : GATE + 768]
    up[0] = g2[:, UP : UP + 768]
    output[0] = g2[:, OUT : OUT + 512]
    down[0] = g2[:, DOWN : DOWN + 768]
    for n, out in enumerate((attn_gain, mlp_gain)):
        row = small[pl.ds(3 * core + n, 1), :]
        own = jnp.zeros((1, BLOCK), F32)
        for index in range(CTX):
            own = jnp.where(here == index, row[:, index * BLOCK : (index + 1) * BLOCK], own)
        out[...] = own
    row = small[pl.ds(3 * core + 2, 1), :]
    query_gain[...] = row[:, 0:128]
    key_gain[...] = row[:, 128:256]


def on_device(
    inputs, positions, cotangent, attn_gain, w_query, w_key, w_value, query_gain, key_gain, w_output,
    mlp_gain, w_gate, w_up, w_down,
):
    w1, w2, kv, *stash = run_forward(
        inputs, positions, attn_gain, w_query, w_key, w_value, query_gain, key_gain,
        jnp.swapaxes(w_output, 1, 2), mlp_gain, w_gate, w_up, jnp.swapaxes(w_down, 1, 2),
    )
    inner, inner_other, outs_other, g1, g2, small = run_backward(w1, w2, kv, inputs, cotangent, *stash)
    outs = dict(zip(STASH, stash))["outs"]
    shapes = [
        ((1, 2, ROWS, WIDTH), BF), ((1, 2, ROWS, WIDTH), F32), ((1, BLOCK), F32), ((1, BLOCK, 512), F32),
        ((1, BLOCK, 256), F32), ((1, BLOCK, 256), F32), ((1, 128), F32), ((1, 128), F32), ((1, BLOCK, 512), F32),
        ((1, BLOCK), F32), ((1, BLOCK, 768), F32), ((1, BLOCK, 768), F32), ((1, BLOCK, 768), F32),
    ]
    results = list(pl.pallas_call(
        results_kernel,
        out_shape=[jax.ShapeDtypeStruct(*shape) for shape in shapes],
        in_specs=[HB] * 7,
        out_specs=[VM] * len(shapes),
        scratch_shapes=[
            *[pltpu.VMEM((ROWS, WIDTH), BF)] * 4,
            pltpu.VMEM((BLOCK, 1024), F32),
            pltpu.VMEM((BLOCK, REST), F32),
            pltpu.VMEM(SMALL, F32),
            DMA((7,)),
        ],
        compiler_params=pltpu.CompilerParams(vmem_limit_bytes=60 * 2**20),
    )(outs, outs_other, inner, inner_other, g1, g2, small))
    for n in (8, 12):
        results[n] = jnp.swapaxes(results[n], 1, 2)
    return tuple(results)


def solution(mesh):
    row, col = P("section", "ctx", "tp"), P("section", "tp", "ctx")
    gain, head = P("section", "ctx"), P("section", None)
    tokens = P(None, "ctx", None)
    layered = P("section", None, "ctx", None)
    return jax.shard_map(
        on_device,
        mesh=mesh,
        in_specs=(tokens, P(None, "ctx"), tokens, gain, row, row, row, head, head, col, gain, row, row, col),
        out_specs=(layered, layered, gain, row, row, row, head, head, col, gain, row, row, col),
        check_vma=False,
    )
```

```python
import math

import jax
import jax.numpy as jnp
import numpy as np
from jax import lax
from jax.experimental import pallas as pl
from jax.experimental.pallas import tpu as pltpu
from jax.sharding import PartitionSpec as P

HEAD_SIZE = 128
EPSILON = 1e-06
ROPE_BASE = 1000000.0
MASKED = -1e30
MESH = pl.DeviceIdType.MESH
BF = jnp.bfloat16
F32 = jnp.float32
CTX = 16
TP = 4
ROWS = 128
SUB = ROWS // TP
WIDTH = 1024
BLOCK = WIDTH // CTX
SCALE = 1.0 / math.sqrt(HEAD_SIZE)


def ring(axis, step, count):
    return lax.rem(lax.axis_index(axis) + step, count)


def remote(src, dst, send, recv, **where):
    return pltpu.make_async_remote_copy(
        src_ref=src, dst_ref=dst, send_sem=send, recv_sem=recv, device_id=where, device_id_type=MESH
    )


def params(collective_id, vmem=48):
    return pltpu.CompilerParams(
        collective_id=collective_id, has_side_effects=True, vmem_limit_bytes=vmem * 2**20
    )


VM = pl.BlockSpec(memory_space=pltpu.VMEM)
HB = pl.BlockSpec(memory_space=pl.ANY)
DMA = pltpu.SemaphoreType.DMA


EDGE = 4
HEADS = 4
FIRST = 1280
REST = 2816
GATE, UP, DOWN, OUT = 0, 768, 1536, 2304
GROUPS = ((0, 0, 1280, 384), (1, 2304, 512, 128), (1, 0, 2304, 640))


def place():
    here = lax.axis_index("ctx")
    return here // EDGE, lax.rem(here, EDGE)


def around(value, step):
    return lax.rem(value + step, EDGE)


def peer_x(step):
    x, y = place()
    return around(x, step) * EDGE + y


def peer_y(step):
    x, y = place()
    return x * EDGE + around(y, step)


def greet_plane():
    sem = pltpu.get_barrier_semaphore()
    for step in range(1, EDGE):
        for where in ({"ctx": peer_x(step)}, {"ctx": peer_y(step)}, {"tp": ring("tp", step, TP)}):
            pl.semaphore_signal(sem, inc=1, device_id=where, device_id_type=MESH)
    pl.semaphore_signal(
        sem, inc=1, device_id={"section": 1 - lax.axis_index("section")}, device_id_type=MESH
    )


def met_plane():
    pl.semaphore_wait(pltpu.get_barrier_semaphore(), 3 * (EDGE - 1) + 1)


class PlaneGather:
    def __init__(self, ref, cols_a, cols_b, send, recv):
        self.ref, self.a, self.b, self.send, self.recv = ref, cols_a, cols_b, send, recv
        self.sent = []

    def push(self, src, slot, peer):
        copy = remote(src, src, self.send.at[slot], self.recv.at[slot], ctx=peer)
        copy.start()
        self.sent.append(copy)

    def wait(self, dst, slot):
        remote(dst, dst, self.send.at[slot], self.recv.at[slot], ctx=lax.axis_index("ctx")).wait_recv()

    def start(self):
        x, y = place()
        for step in range(1, EDGE):
            self.push(self.ref.at[x, y, :, self.a], step - 1, peer_x(step))
            self.push(self.ref.at[x, y, :, self.b], step + 2, peer_y(step))

    def middle(self):
        x, y = place()
        for step in range(1, EDGE):
            self.wait(self.ref.at[around(x, EDGE - step), y, :, self.a], step - 1)
        for step in range(1, EDGE):
            self.push(self.ref.at[:, y, :, self.a], step + 5, peer_y(step))
        for step in range(1, EDGE):
            self.wait(self.ref.at[x, around(y, EDGE - step), :, self.b], step + 2)
        for step in range(1, EDGE):
            self.push(self.ref.at[x, :, :, self.b], step + 8, peer_x(step))

    def second(self):
        x, y = place()
        for step in range(1, EDGE):
            yield self.ref.at[:, around(y, EDGE - step), :, self.a], step + 5
            yield self.ref.at[around(x, EDGE - step), :, :, self.b], step + 8

    def end(self):
        for dst, slot in self.second():
            self.wait(dst, slot)

    def finish(self):
        finish(self.sent)


class KeyGather(PlaneGather):
    def start(self):
        x, y = place()
        for step in (1, 3, 2):
            self.push(self.ref.at[x, y, :, self.a], step - 1, peer_x(step))
            self.push(self.ref.at[x, y, :, self.b], step + 14, peer_y(step))
        for step in (1, 3, 2):
            self.push(self.ref.at[x, y, :, self.a], step + 2, peer_y(step))
            self.push(self.ref.at[x, y, :, self.b], step + 17, peer_x(step))

    def middle(self):
        x, y = place()
        for step in (1, 3, 2):
            block = self.ref.at[around(x, EDGE - step), y, :, self.a]
            self.wait(block, step - 1)
            for to in (1, 3, 2):
                self.push(block, 3 * step + to + 2, peer_y(to))
            block = self.ref.at[x, around(y, EDGE - step), :, self.b]
            self.wait(block, step + 14)
            for to in (1, 3, 2):
                self.push(block, 3 * step + to + 17, peer_x(to))

    def end(self):
        x, y = place()
        for to in (1, 3, 2):
            self.wait(self.ref.at[x, around(y, EDGE - to), :, self.a], to + 2)
            self.wait(self.ref.at[around(x, EDGE - to), y, :, self.b], to + 17)
        for step in (1, 3, 2):
            for to in (1, 3, 2):
                self.wait(self.ref.at[around(x, EDGE - step), around(y, EDGE - to), :, self.a], 3 * step + to + 2)
                self.wait(self.ref.at[around(x, EDGE - to), around(y, EDGE - step), :, self.b], 3 * step + to + 17)


class WeightGather(PlaneGather):
    def __init__(self, ref, low, width, first, send, recv, pair_send, pair_recv):
        half = width // 2

        def cols(core):
            start = pl.multiple_of(low + core * half, 128)
            return pl.ds(start, first), pl.ds(pl.multiple_of(start + first, 128), half - first)

        core = lax.axis_index("section")
        super().__init__(ref, *cols(core), send, recv)
        self.theirs = cols(1 - core)
        self.pair_send, self.pair_recv = pair_send, pair_recv

    def hand(self, src, slot):
        other = 1 - lax.axis_index("section")
        copy = remote(src, src, self.pair_send.at[slot], self.pair_recv.at[slot], section=other)
        copy.start()
        self.sent.append(copy)

    def taken(self, dst, slot):
        here = lax.axis_index("section")
        remote(dst, dst, self.pair_send.at[slot], self.pair_recv.at[slot], section=here).wait_recv()

    def middle(self):
        super().middle()
        x, y = place()
        self.hand(self.ref.at[:, y, :, self.a], 0)
        self.hand(self.ref.at[x, :, :, self.b], 1)

    def end(self):
        x, y = place()
        for n, (dst, slot) in enumerate(self.second()):
            self.wait(dst, slot)
            self.hand(dst, n + 2)
        a, b = self.theirs
        self.taken(self.ref.at[:, y, :, a], 0)
        self.taken(self.ref.at[x, :, :, b], 1)
        for step in range(1, EDGE):
            self.taken(self.ref.at[:, around(y, EDGE - step), :, a], 2 * step)
            self.taken(self.ref.at[around(x, EDGE - step), :, :, b], 2 * step + 1)


def mm(a, b, contract=(1, 0)):
    return lax.dot_general(a, b, (((contract[0],), (contract[1],)), ((), ())), preferred_element_type=F32)


def flat(ref, layer, low, size):
    value = ref[layer, :, :, :, low : low + size]
    return value.reshape(-1, size)


def unit_rms(values):
    return values * lax.rsqrt(jnp.mean(values * values, -1, keepdims=True) + EPSILON)


def head(value, index):
    return value[:, index * HEAD_SIZE : (index + 1) * HEAD_SIZE]


def turn(values, gain, cos, sin):
    outs = []
    for index in range(values.shape[1] // HEAD_SIZE):
        scaled = unit_rms(head(values, index)) * gain
        outs.append(scaled * cos + pltpu.roll(scaled, HEAD_SIZE // 2, 1) * sin)
    return jnp.concatenate(outs, 1).astype(BF)


def scores_t(keys, query, first):
    raw = mm(keys, query, (1, 1)) * SCALE
    rows = lax.broadcasted_iota(jnp.int32, raw.shape, 0)
    last = lax.axis_index("ctx") * ROWS + lax.broadcasted_iota(jnp.int32, (1, ROWS), 1)
    return jnp.where((rows <= last) & (rows >= first), raw, MASKED)


def forward_layer(layer, hidden, w1, w2, first, cos, sin, st, tp_sems, keys_gather, groups, following):
    here = lax.axis_index("tp")
    x, y = place()
    rows = pl.ds(pl.multiple_of(here * SUB, SUB), SUB)
    part, landing = st["part"], st["landing"]
    groups[0].end()
    gains = flat(w1, layer, 1024, 128).astype(F32).T[:8]
    st["gains"][layer] = gains
    heads = w1[layer, 0, 0, 0:16, 1152:1280].astype(F32)
    st["head_gains"][layer] = heads[:8]
    normed = (unit_rms(hidden[...].astype(F32)) * gains[0:1]).astype(BF)
    st["normed"][layer] = normed
    key_proj = mm(normed, flat(w1, layer, 512, 256))
    value = mm(normed, flat(w1, layer, 768, 256))
    st["key_proj"][layer] = key_proj
    kv = st["kv"]
    kv[layer, x, y, :, 0:256] = turn(key_proj, heads[1:2], cos, sin)
    kv[layer, x, y, :, 256:512] = value.astype(BF)
    keys_gather.start()
    query_proj = mm(normed, flat(w1, layer, 0, 512))
    st["query_proj"][layer] = query_proj
    query = turn(query_proj, heads[0:1], cos, sin)
    st["query"][layer] = query
    st["keep"](0, layer)
    keys_gather.middle()
    if following:
        groups[1].middle()
    keys_gather.end()
    st["keep"](2, layer)
    groups[2].middle()
    mixed = []
    for group in range(2):
        keys = flat(kv, layer, group * HEAD_SIZE, HEAD_SIZE)
        values_t = flat(kv, layer, 256 + group * HEAD_SIZE, HEAD_SIZE).T
        for index in (2 * group, 2 * group + 1):
            scores = scores_t(keys, head(query, index), first)
            top = jnp.max(scores, 0, keepdims=True)
            raised = jnp.exp(scores - top)
            total = jnp.sum(raised, 0, keepdims=True)
            low = (raised * (1.0 / total)).astype(BF)
            st["level"][layer, index : index + 1, :] = top + jnp.log(total)
            mixed.append(mm(values_t, low).T.astype(BF))
    mixed = jnp.concatenate(mixed, 1)
    st["mixed"][layer] = mixed
    groups[1].end()
    part[2 * layer] = mm(mixed, flat(w2, layer, OUT, 512), (1, 1)).astype(BF)
    sems = [s.at[2 * layer] for s in tp_sems]
    sent = tp_scatter(part.at[2 * layer], landing.at[2 * layer], sems[0], sems[1])
    if following:
        following[0].start()
    total = tp_total(part.at[2 * layer], landing.at[2 * layer], sent)
    after = total + hidden[rows, :].astype(F32)
    st["after"][layer] = after
    mlp_in = st["mlp_in"].at[layer]
    mlp_in[rows, :] = (unit_rms(after) * gains[1:2]).astype(BF)
    sent += tp_spread(mlp_in, sems[2], sems[3])
    if following:
        following[0].middle()
    groups[2].end()
    tp_spread_wait(mlp_in, sems[2], sems[3])
    gate = mm(mlp_in[...], flat(w2, layer, GATE, 768))
    up = mm(mlp_in[...], flat(w2, layer, UP, 768))
    st["gate"][layer] = gate
    st["up"][layer] = up
    st["keep"](1, layer)
    if following is None:
        return sent
    activated = (gate / (1.0 + jnp.exp(-gate)) * up).astype(BF)
    for group in following[1:]:
        group.start()
    part[2 * layer + 1] = mm(activated, flat(w2, layer, DOWN, 768), (1, 1)).astype(BF)
    sems = [s.at[2 * layer + 1] for s in tp_sems]
    copies = tp_scatter(part.at[2 * layer + 1], landing.at[2 * layer + 1], sems[0], sems[1])
    total = tp_total(part.at[2 * layer + 1], landing.at[2 * layer + 1], copies)
    out = st["outs"].at[layer]
    out[rows, :] = (total + after).astype(BF)
    copies += tp_spread(out, sems[2], sems[3])
    following[1].middle()
    tp_spread_wait(out, sems[2], sems[3])
    return sent + copies


STASH = dict(
    first=((1, ROWS), jnp.int32),
    cos=((ROWS, HEAD_SIZE), F32),
    sin=((ROWS, HEAD_SIZE), F32),
    normed=((2, ROWS, WIDTH), BF),
    query_proj=((2, ROWS, 512), F32),
    key_proj=((2, ROWS, 256), F32),
    query=((2, ROWS, 512), BF),
    level=((2, 8, ROWS), F32),
    mixed=((2, ROWS, 512), BF),
    after=((2, SUB, WIDTH), F32),
    mlp_in=((2, ROWS, WIDTH), BF),
    gate=((2, ROWS, 768), F32),
    up=((2, ROWS, 768), F32),
    outs=((1, ROWS, WIDTH), BF),
    gains=((2, 8, WIDTH), F32),
    head_gains=((2, 8, HEAD_SIZE), F32),
)
KEPT = [
    ((2, EDGE, EDGE, BLOCK, FIRST), BF),
    ((2, EDGE, EDGE, BLOCK, REST), BF),
    ((2, EDGE, EDGE, ROWS, 512), BF),
]


def forward_kernel(
    inputs, positions, attn_gain, w_query, w_key, w_value, query_gain, key_gain, w_output, mlp_gain, w_gate, w_up,
    w_down, speeds, w1_out, w2_out, kv_out, *refs
):
    st = dict(zip(STASH, refs))
    own1, own2, w1, w2, st["kv"], st["part"], st["landing"], *refs = refs[len(STASH) :]
    tp_sems, (local, swap_send, swap_recv, send, recv, pair_send, pair_recv, kv_send, kv_recv, keep) = refs[:4], refs[4:]
    core = lax.axis_index("section")
    other = 1 - core
    x, y = place()
    kept = []

    def keep_copy(n, layer):
        src, dst = ((w1, w1_out), (w2, w2_out), (st["kv"], kv_out))[n]
        kept.append(pltpu.make_async_copy(src.at[layer], dst.at[layer], keep.at[layer, n]))
        kept[-1].start()

    st["keep"] = keep_copy
    gathers = [
        [
            WeightGather((w1, w2)[which].at[layer], low, width, along_x, send.at[layer, n], recv.at[layer, n],
                         pair_send.at[layer, n], pair_recv.at[layer, n])
            for n, (which, low, width, along_x) in enumerate(GROUPS)
        ]
        for layer in range(2)
    ]
    greet_plane()
    own1[:, 0:512] = w_query[0]
    own1[:, 512:768] = w_key[0]
    own1[:, 768:1024] = w_value[0]
    tail = [attn_gain[...].astype(F32), mlp_gain[...].astype(F32), jnp.zeros((126, BLOCK), F32)]
    own1[:, 1024:1152] = jnp.concatenate(tail, 0).T.astype(BF)
    tail = [query_gain[...].astype(F32), key_gain[...].astype(F32), jnp.zeros((BLOCK - 2, HEAD_SIZE), F32)]
    own1[:, 1152:1280] = jnp.concatenate(tail, 0).astype(BF)
    own2[:, GATE : GATE + 768] = w_gate[0]
    own2[:, UP : UP + 768] = w_up[0]
    own2[:, OUT : OUT + 512] = w_output[0]
    own2[:, DOWN : DOWN + 768] = w_down[0]
    met_plane()
    swaps, locals_ = [], []
    for n, (own, ref) in enumerate(((own1, w1), (own2, w2))):
        for low, width in [(g[1], g[2]) for g in GROUPS if g[0] == n]:
            slot = len(swaps)
            half = width // 2
            cut = pl.ds(pl.multiple_of(low + other * half, 128), half)
            mine = pl.ds(pl.multiple_of(low + core * half, 128), half)
            swaps.append(
                remote(own.at[:, cut], ref.at[core, x, y, :, cut], swap_send.at[slot], swap_recv.at[slot], section=other)
            )
            swaps[-1].start()
            locals_.append(pltpu.make_async_copy(own.at[:, mine], ref.at[core, x, y, :, mine], local.at[slot]))
            locals_[-1].start()
    for slot, (n, low, width, _) in enumerate(GROUPS):
        half = width // 2
        dst = (w1, w2)[n].at[other, x, y, :, pl.ds(pl.multiple_of(low + core * half, 128), half)]
        locals_[slot].wait()
        remote(dst, dst, swap_send.at[slot], swap_recv.at[slot], section=core).wait_recv()
        if slot == 0:
            gathers[0][0].start()
    gathers[0][0].middle()
    for group in gathers[0][1:]:
        group.start()
    keys = [
        KeyGather(st["kv"].at[layer], pl.ds(0, 256), pl.ds(256, 256), kv_send.at[layer], kv_recv.at[layer])
        for layer in range(2)
    ]
    token_pos = positions[pl.ds(core, 1), :]
    first = lax.axis_index("ctx") * ROWS + lax.broadcasted_iota(jnp.int32, (1, ROWS), 1) - token_pos
    angles = jnp.broadcast_to(token_pos.astype(F32), (ROWS, ROWS)).T * speeds[...]
    cos, sin = jnp.cos(angles), jnp.sin(angles)
    low_half = lax.broadcasted_iota(jnp.int32, (ROWS, HEAD_SIZE), 1) < HEAD_SIZE // 2
    tables = first, cos, jnp.where(low_half, -sin, sin)
    for name, table in zip(("first", "cos", "sin"), tables):
        st[name][...] = table
    sent = forward_layer(0, inputs.at[core], w1, w2, *tables, st, tp_sems, keys[0], gathers[0], gathers[1])
    sent += forward_layer(1, st["outs"].at[0], w1, w2, *tables, st, tp_sems, keys[1], gathers[1], None)
    finish(sent + swaps)
    for part in keys + gathers[0] + gathers[1]:
        part.finish()
    for copy in kept:
        copy.wait()


def run_forward(*args):
    outs = KEPT + list(STASH.values())
    speeds = ROPE_BASE ** (-(np.arange(HEAD_SIZE // 2, dtype=np.float32) * np.float32(2.0 / HEAD_SIZE)))
    speeds = jnp.asarray(np.tile(speeds, 2)[None].astype(np.float32))
    return pl.pallas_call(
        forward_kernel,
        out_shape=[jax.ShapeDtypeStruct(*o) for o in outs],
        in_specs=[VM] * (len(args) + 1),
        out_specs=[HB] * 3 + [VM] * len(STASH),
        scratch_shapes=[
            pltpu.VMEM((BLOCK, FIRST), BF),
            pltpu.VMEM((BLOCK, REST), BF),
            *[pltpu.VMEM(*k) for k in KEPT],
            pltpu.VMEM((4, ROWS, WIDTH), BF),
            pltpu.VMEM((4, TP - 1, SUB, WIDTH), BF),
            *[DMA((4, TP - 1))] * 4,
            DMA((3,)), DMA((3,)), DMA((3,)),
            DMA((2, 3, 12)), DMA((2, 3, 12)), DMA((2, 3, 8)), DMA((2, 3, 8)), DMA((2, 30)), DMA((2, 30)), DMA((2, 3)),
        ],
        compiler_params=params(1, 60),
    )(*args, speeds)


def tp_rows(ref, index):
    return ref.at[pl.ds(pl.multiple_of(index * SUB, SUB), SUB)]


def tp_scatter(part, landing, send, recv):
    copies = []
    for step in (2, 1, 3):
        peer = ring("tp", step, TP)
        copies.append(
            remote(tp_rows(part, peer), landing.at[step - 1], send.at[step - 1], recv.at[step - 1], tp=peer)
        )
        copies[-1].start()
    return copies


def tp_total(part, landing, copies):
    total = tp_rows(part, lax.axis_index("tp"))[...].astype(F32)
    for copy in copies:
        copy.wait_recv()
    for step in range(TP - 1):
        total = total + landing[step].astype(F32)
    return total


def tp_spread(full, send, recv):
    here = lax.axis_index("tp")
    copies = []
    for step in (2, 1, 3):
        rows = tp_rows(full, here)
        copies.append(remote(rows, rows, send.at[step - 1], recv.at[step - 1], tp=ring("tp", step, TP)))
        copies[-1].start()
    return copies


def tp_spread_wait(full, send, recv):
    here = lax.axis_index("tp")
    for step in range(TP - 1):
        rows = tp_rows(full, ring("tp", TP - 1 - step, TP))
        remote(rows, rows, send.at[step], recv.at[step], tp=here).wait_recv()


def finish(copies):
    for copy in copies:
        copy.wait_send()


def norm_back(values, grad, gain):
    inverse = lax.rsqrt(jnp.mean(values * values, -1, keepdims=True) + EPSILON)
    unit = values * inverse
    scaled = grad * gain
    back = inverse * (scaled - unit * jnp.mean(scaled * unit, -1, keepdims=True))
    return back, jnp.sum(grad * unit, 0, keepdims=True)


class PlaneScatter:
    def __init__(self, ref, cols_a, cols_b, lands, send, recv):
        self.ref, self.a, self.b, self.send, self.recv = ref, cols_a, cols_b, send, recv
        self.lands = lands
        self.sent = []

    def push(self, src, land, slot, peer):
        copy = remote(src, land, self.send.at[slot], self.recv.at[slot], ctx=peer)
        copy.start()
        self.sent.append(copy)

    def add(self, own, phase, slot):
        land = self.lands[phase]
        for step in range(EDGE - 1):
            dst = land.at[step]
            sems = self.send.at[slot + step], self.recv.at[slot + step]
            remote(dst, dst, *sems, ctx=lax.axis_index("ctx")).wait_recv()
        total = own[...].astype(F32)
        for step in range(EDGE - 1):
            total = total + land[step].astype(F32)
        return total

    def start(self):
        x, y = place()
        for step in range(1, EDGE):
            self.push(self.ref.at[around(x, step), :, :, self.a], self.lands[0].at[step - 1], step - 1, peer_x(step))
            self.push(self.ref.at[:, around(y, step), :, self.b], self.lands[1].at[step - 1], step + 2, peer_y(step))

    def middle(self):
        x, y = place()
        own = self.ref.at[x, :, :, self.a]
        own[...] = self.add(own, 0, 0).astype(BF)
        for step in range(1, EDGE):
            self.push(self.ref.at[x, around(y, step), :, self.a], self.lands[2].at[step - 1], step + 5, peer_y(step))
        own = self.ref.at[:, y, :, self.b]
        own[...] = self.add(own, 1, 3).astype(BF)
        for step in range(1, EDGE):
            self.push(self.ref.at[around(x, step), y, :, self.b], self.lands[3].at[step - 1], step + 8, peer_x(step))

    def end(self):
        x, y = place()
        return self.add(self.ref.at[x, y, :, self.a], 2, 6), self.add(self.ref.at[x, y, :, self.b], 3, 9)

    def finish(self):
        finish(self.sent)


GRAD_HALF = {1024: (256, 256), REST: (768, 640)}


def scatter_lands(rows, first, second):
    return [
        ((EDGE - 1, EDGE, rows, first), BF),
        ((EDGE - 1, EDGE, rows, second), BF),
        ((EDGE - 1, rows, first), BF),
        ((EDGE - 1, rows, second), BF),
    ]


class GradScatter(PlaneScatter):
    def __init__(self, ref, lands, send, recv, pair_land, pair_send, pair_recv):
        half = ref.shape[-1] // 2
        first, second = GRAD_HALF[ref.shape[-1]]
        core = lax.axis_index("section")
        low = pl.multiple_of(core * half, 128)
        super().__init__(ref, pl.ds(low, first), pl.ds(pl.multiple_of(low + first, 128), second), lands, send, recv)
        self.mine = pl.ds(low, half)
        self.theirs = pl.ds(pl.multiple_of((1 - core) * half, 128), half)
        self.pair_land = pair_land
        self.pair = remote(ref.at[:, :, :, self.theirs], pair_land, pair_send, pair_recv, section=1 - core)
        self.half, self.first = half, first

    def swap(self):
        self.pair.start()

    def start(self):
        self.pair.wait_recv()
        for row in range(EDGE):
            own = self.ref.at[row, :, :, self.mine]
            own[...] = (own[...].astype(F32) + self.pair_land[row].astype(F32)).astype(BF)
        super().start()

    def finish(self):
        self.pair.wait_send()
        super().finish()

    def result(self, out):
        a, b = self.end()
        out[:, self.a] = a
        out[:, self.b] = b


def weight_grad(ref, low, left_t, right):
    size = right.shape[1]
    for row in range(EDGE):
        block = mm(left_t[row * 256 : (row + 1) * 256], right)
        ref[row, :, :, low : low + size] = block.reshape(EDGE, BLOCK, size).astype(BF)


def turn_back(grads, values, gain, cos, sin):
    outs, terms = [], 0.0
    for index in range(values.shape[1] // HEAD_SIZE):
        grad = head(grads, index)
        grad = grad * cos + pltpu.roll(grad * sin, HEAD_SIZE // 2, 1)
        back, term = norm_back(head(values, index), grad, gain)
        outs.append(back.astype(BF))
        terms = terms + term
    return jnp.concatenate(outs, 1), terms


def wide(buf, low, size):
    return buf[:, :, :, low : low + size].reshape(-1, size)


BACK_IN = ("inputs", "cotangent")
BACK_KEPT = [(EDGE, EDGE, BLOCK, 1024), *[k[0][1:] for k in KEPT[1:]]]
SMALL = (8, WIDTH)
LANDS = [
    *scatter_lands(BLOCK, *GRAD_HALF[REST]), *scatter_lands(BLOCK, *GRAD_HALF[1024]), *scatter_lands(ROWS, 256, 256)
]


def backward_kernel(w1_all, w2_all, kv_all, *refs):
    names = (*BACK_IN, *STASH)
    st = dict(zip(names, refs))
    inner, inner_other, outs, outs_other, g1_out, g2_out, small_out, *refs = refs[len(names) :]
    w1, w2, kv, dkv, g1, g2, res1, res2, pair1, pair2, part, landing, middle_grad, small, small_land, *refs = refs
    lands = [refs[n * len(LANDS) : (n + 1) * len(LANDS)] for n in range(2)]
    refs = refs[2 * len(LANDS) :]
    tp_sems, (load, send, recv, pair_send, pair_recv, small_send, small_recv, end_send, end_recv) = refs[:4], refs[4:]
    core = lax.axis_index("section")
    other = 1 - core
    here = lax.axis_index("tp")
    x, y = place()
    cos, sin, first = st["cos"][...], st["sin"][...], st["first"][...]
    sent = []
    loads = [
        [pltpu.make_async_copy(src, dst, load.at[layer, n])
         for n, (src, dst) in enumerate(
             ((w1_all.at[layer, :, :, :, 0:1024], w1), (w2_all.at[layer], w2), (kv_all.at[layer], kv)))]
        for layer in range(2)
    ]
    greet_plane()
    for n in (1, 2, 0):
        loads[1][n].start()
    rest = [
        GradScatter(g2.at[layer], lands[layer][0:4], send.at[layer, 0], recv.at[layer, 0],
                    pair2.at[layer], pair_send.at[layer, 0], pair_recv.at[layer, 0])
        for layer in range(2)
    ]
    head_grads = [
        GradScatter(g1, lands[layer][4:8], send.at[layer, 1], recv.at[layer, 1],
                    pair1.at[layer], pair_send.at[layer, 1], pair_recv.at[layer, 1])
        for layer in range(2)
    ]
    keys = [
        PlaneScatter(dkv, pl.ds(0, 256), pl.ds(256, 256), lands[layer][8:12], send.at[layer, 2], recv.at[layer, 2])
        for layer in range(2)
    ]
    small[...] = jnp.zeros(SMALL, F32)
    met_plane()
    outs[0] = st["outs"][0]
    ends = [remote(outs.at[other], outs_other, end_send.at[3], end_recv.at[3], section=other)]
    last_sems = [s.at[4] for s in tp_sems]
    rows = pl.ds(pl.multiple_of(here * SUB, SUB), SUB)
    def small_round(slot, peers):
        copies = []
        for n, where in enumerate(peers):
            copies.append(
                remote(small, small_land.at[slot + n], small_send.at[slot + n], small_recv.at[slot + n], **where)
            )
            copies[-1].start()
        return copies

    def small_add(slot, copies):
        for copy in copies:
            copy.wait()
        small[...] += sum(small_land[slot + n] for n in range(len(copies)))

    out_grad = st["cotangent"].at[core]
    for layer in (1, 0):
        hidden = st["outs"].at[0] if layer else st["inputs"].at[core]
        gains, head_gains = st["gains"][layer], st["head_gains"][layer]
        sems = [[s.at[2 * layer + n] for s in tp_sems] for n in range(2)]
        grad_low = out_grad[...]
        grad_rows = out_grad[rows, :].astype(F32)
        gate, up = st["gate"][layer], st["up"][layer]
        sigmoid = 1.0 / (1.0 + jnp.exp(-gate))
        loads[layer][1].wait()
        act_grad = mm(grad_low, wide(w2, DOWN, 768))
        gate_low = (act_grad * up * sigmoid * (1.0 + gate * (1.0 - sigmoid))).astype(BF)
        up_low = (act_grad * gate * sigmoid).astype(BF)
        activated = (gate * sigmoid * up).astype(BF)
        part[2 * layer] = (
            mm(gate_low, wide(w2, GATE, 768), (1, 1)) + mm(up_low, wide(w2, UP, 768), (1, 1))
        ).astype(BF)
        copies = tp_scatter(part.at[2 * layer], landing.at[2 * layer], *sems[0][:2])
        if layer == 0:
            rest[1].middle()
            head_grads[1].start()
        else:
            part[4] = mm(activated, wide(w2, DOWN, 768), (1, 1)).astype(BF)
        mlp_t = st["mlp_in"][layer].T
        weight_grad(g2.at[layer], GATE, mlp_t, gate_low)
        weight_grad(g2.at[layer], UP, mlp_t, up_low)
        total = tp_total(part.at[2 * layer], landing.at[2 * layer], copies)
        sent += copies
        back, terms = norm_back(st["after"][layer], total, gains[1:2])
        small[3 * layer + 1 : 3 * layer + 2, :] = terms
        grad_rows = grad_rows + back
        full = middle_grad.at[layer]
        tp_rows(full, here)[...] = grad_rows.astype(BF)
        sent += tp_spread(full, *sems[0][2:])
        weight_grad(g2.at[layer], DOWN, grad_low.T, activated)
        if layer == 0:
            rest[1].result(res2.at[1])
        else:
            last = tp_scatter(part.at[4], landing.at[4], *last_sems[:2])
        tp_spread_wait(full, *sems[0][2:])
        grad_low = full[...]
        mixed_grad = mm(grad_low, wide(w2, OUT, 512)).astype(BF)
        if layer == 1:
            loads[0][1].start()
        weight_grad(g2.at[layer], OUT, grad_low.T, st["mixed"][layer])
        rest[layer].swap()
        if layer == 1:
            total = tp_total(part.at[4], landing.at[4], last)
            outs[1, rows, :] = (total + st["after"][1]).astype(BF)
            sent += last + tp_spread(outs.at[1], *last_sems[2:])
        loads[layer][2].wait()
        query = st["query"][layer]
        query_grads = []
        if layer == 0:
            head_grads[1].middle()
        for group in range(2):
            group_keys = wide(kv, group * HEAD_SIZE, HEAD_SIZE)
            group_values = wide(kv, 256 + group * HEAD_SIZE, HEAD_SIZE)
            keys_t = group_keys.T
            key_grad, value_grad = 0.0, 0.0
            for index in (2 * group, 2 * group + 1):
                head_query, head_grad = head(query, index), head(mixed_grad, index)
                scores = scores_t(group_keys, head_query, first)
                prob = jnp.exp(scores - st["level"][layer, index : index + 1, :])
                prob_grad = mm(group_values, head_grad, (1, 1))
                dots = jnp.sum(prob * prob_grad, 0, keepdims=True)
                score_low = (prob * (prob_grad - dots)).astype(BF)
                query_grads.append(mm(keys_t, score_low).T * SCALE)
                key_grad = key_grad + mm(score_low, head_query)
                value_grad = value_grad + mm(prob.astype(BF), head_grad)
            shape = (EDGE, EDGE, ROWS, HEAD_SIZE)
            dkv[:, :, :, group * HEAD_SIZE : (group + 1) * HEAD_SIZE] = (key_grad * SCALE).astype(BF).reshape(shape)
            low = 256 + group * HEAD_SIZE
            dkv[:, :, :, low : low + HEAD_SIZE] = value_grad.astype(BF).reshape(shape)
        keys[layer].start()
        if layer == 1:
            loads[0][2].start()
            tp_spread_wait(outs.at[1], *last_sems[2:])
            ends[0].start()
        query_low, terms = turn_back(
            jnp.concatenate(query_grads, 1), st["query_proj"][layer], head_gains[0:1], cos, sin
        )
        small[3 * layer + 2 : 3 * layer + 3, 0:128] = terms
        normed_t = st["normed"][layer].T
        if layer == 0:
            head_grads[1].result(res1.at[1])
            head_grads[1].finish()
        keys[layer].middle()
        rest[layer].start()
        weight_grad(g1, 0, normed_t, query_low)
        key_grad, value_grad = keys[layer].end()
        keys[layer].finish()
        key_low, terms = turn_back(key_grad, st["key_proj"][layer], head_gains[1:2], cos, sin)
        small[3 * layer + 2 : 3 * layer + 3, 128:256] = terms
        joined = jnp.concatenate([query_low, key_low, value_grad.astype(BF)], 1)
        loads[layer][0].wait()
        part[2 * layer + 1] = mm(joined, wide(w1, 0, 1024), (1, 1)).astype(BF)
        if layer == 1:
            loads[0][0].start()
        copies = tp_scatter(part.at[2 * layer + 1], landing.at[2 * layer + 1], *sems[1][:2])
        weight_grad(g1, 512, normed_t, joined[:, 512:])
        head_grads[layer].swap()
        total = tp_total(part.at[2 * layer + 1], landing.at[2 * layer + 1], copies)
        sent += copies
        back, terms = norm_back(hidden[rows, :].astype(F32), total, gains[0:1])
        small[3 * layer : 3 * layer + 1, :] = terms
        full = inner.at[layer]
        tp_rows(full, here)[...] = (grad_rows + back).astype(BF)
        sent += tp_spread(full, *sems[1][2:])
        if layer == 0:
            around_pair = small_round(0, [dict(section=other)])
            head_grads[0].start()
        tp_spread_wait(full, *sems[1][2:])
        out_grad = full
    ends.append(remote(inner.at[other], inner_other, end_send.at[0], end_recv.at[0], section=other))
    ends[1].start()

    steps = range(1, EDGE)

    def deliver(n, grad, res, out):
        grad.result(res.at[0])
        part_out = res.at[other, :, grad.mine]
        ends.append(remote(part_out, out.at[:, grad.mine], end_send.at[n], end_recv.at[n], section=other))
        ends[-1].start()
        out[:, grad.mine] = res[core, :, grad.mine]

    small_add(0, around_pair)
    around_x = small_round(1, [dict(ctx=peer_x(step)) for step in steps])
    rest[0].middle()
    small_add(1, around_x)
    around_y = small_round(4, [dict(ctx=peer_y(step)) for step in steps])
    head_grads[0].middle()
    small_add(4, around_y)
    around_z = small_round(7, [dict(tp=ring("tp", step, TP)) for step in steps])
    deliver(2, rest[0], res2, g2_out)
    deliver(1, head_grads[0], res1, g1_out)
    small_add(7, around_z)
    small_out[...] = small[...]
    ends[0].wait_recv()
    ends[1].wait_recv()
    for n, grad, out in ((2, rest[0], g2_out), (1, head_grads[0], g1_out)):
        dst = out.at[:, grad.theirs]
        remote(dst, dst, end_send.at[n], end_recv.at[n], section=core).wait_recv()
    finish(ends + sent)
    for grad in (*rest, head_grads[0]):
        grad.finish()


def run_backward(w1, w2, kv, *args):
    outs = [
        ((2, ROWS, WIDTH), BF), ((ROWS, WIDTH), BF), ((2, ROWS, WIDTH), BF), ((ROWS, WIDTH), BF), ((BLOCK, 1024), F32), ((BLOCK, REST), F32), (SMALL, F32),
    ]
    return pl.pallas_call(
        backward_kernel,
        out_shape=[jax.ShapeDtypeStruct(*o) for o in outs],
        in_specs=[HB] * 3 + [VM] * len(args),
        out_specs=[VM, HB, VM, HB, VM, VM, VM],
        scratch_shapes=[
            *[pltpu.VMEM(k, BF) for k in BACK_KEPT],
            pltpu.VMEM((EDGE, EDGE, ROWS, 512), BF),
            pltpu.VMEM((EDGE, EDGE, BLOCK, 1024), BF),
            pltpu.VMEM((2, EDGE, EDGE, BLOCK, REST), BF),
            pltpu.VMEM((2, BLOCK, 1024), F32),
            pltpu.VMEM((2, BLOCK, REST), F32),
            pltpu.VMEM((2, EDGE, EDGE, BLOCK, 512), BF),
            pltpu.VMEM((2, EDGE, EDGE, BLOCK, REST // 2), BF),
            pltpu.VMEM((5, ROWS, WIDTH), BF),
            pltpu.VMEM((5, TP - 1, SUB, WIDTH), BF),
            pltpu.VMEM((2, ROWS, WIDTH), BF),
            pltpu.VMEM(SMALL, F32),
            pltpu.VMEM((10, *SMALL), F32),
            *[pltpu.VMEM(*k) for k in LANDS * 2],
            *[DMA((5, TP - 1))] * 4,
            DMA((2, 3)), DMA((2, 3, 12)), DMA((2, 3, 12)), DMA((2, 2)), DMA((2, 2)),
            DMA((10,)), DMA((10,)), DMA((4,)), DMA((4,)),
        ],
        compiler_params=params(2, 62),
    )(w1, w2, kv, *args)


def results_kernel(
    outs_all, outs_other_all, inner_all, inner_other_all, g1_all, g2_all, small_all, section_out, input_grad,
    attn_gain, query, key, value, query_gain, key_gain, output, mlp_gain, gate, up, down, *refs
):
    core, here = lax.axis_index("section"), lax.axis_index("ctx")
    loads = [
        pltpu.make_async_copy(src, dst, refs[-1].at[n])
        for n, (src, dst) in enumerate(
            zip(
                (outs_all.at[core], outs_other_all, inner_all.at[core], inner_other_all, g1_all, g2_all, small_all),
                refs[:-1],
            )
        )
    ]
    for load in loads:
        load.start()
    outs, outs_other, inner, inner_other, g1, g2, small = refs[:-1]
    for load in loads:
        load.wait()
    section_out[0, core] = outs[...]
    section_out[0, 1 - core] = outs_other[...]
    input_grad[0, core] = inner[...].astype(F32)
    input_grad[0, 1 - core] = inner_other[...].astype(F32)
    query[0] = g1[:, 0:512]
    key[0] = g1[:, 512:768]
    value[0] = g1[:, 768:1024]
    gate[0] = g2[:, GATE : GATE + 768]
    up[0] = g2[:, UP : UP + 768]
    output[0] = g2[:, OUT : OUT + 512]
    down[0] = g2[:, DOWN : DOWN + 768]
    for n, out in enumerate((attn_gain, mlp_gain)):
        row = small[pl.ds(3 * core + n, 1), :]
        own = jnp.zeros((1, BLOCK), F32)
        for index in range(CTX):
            own = jnp.where(here == index, row[:, index * BLOCK : (index + 1) * BLOCK], own)
        out[...] = own
    row = small[pl.ds(3 * core + 2, 1), :]
    query_gain[...] = row[:, 0:128]
    key_gain[...] = row[:, 128:256]


def on_device(
    inputs, positions, cotangent, attn_gain, w_query, w_key, w_value, query_gain, key_gain, w_output,
    mlp_gain, w_gate, w_up, w_down,
):
    w1, w2, kv, *stash = run_forward(
        inputs, positions, attn_gain, w_query, w_key, w_value, query_gain, key_gain,
        jnp.swapaxes(w_output, 1, 2), mlp_gain, w_gate, w_up, jnp.swapaxes(w_down, 1, 2),
    )
    inner, inner_other, outs, outs_other, g1, g2, small = run_backward(w1, w2, kv, inputs, cotangent, *stash)
    shapes = [
        ((1, 2, ROWS, WIDTH), BF), ((1, 2, ROWS, WIDTH), F32), ((1, BLOCK), F32), ((1, BLOCK, 512), F32),
        ((1, BLOCK, 256), F32), ((1, BLOCK, 256), F32), ((1, 128), F32), ((1, 128), F32), ((1, BLOCK, 512), F32),
        ((1, BLOCK), F32), ((1, BLOCK, 768), F32), ((1, BLOCK, 768), F32), ((1, BLOCK, 768), F32),
    ]
    results = list(pl.pallas_call(
        results_kernel,
        out_shape=[jax.ShapeDtypeStruct(*shape) for shape in shapes],
        in_specs=[HB] * 7,
        out_specs=[VM] * len(shapes),
        scratch_shapes=[
            *[pltpu.VMEM((ROWS, WIDTH), BF)] * 4,
            pltpu.VMEM((BLOCK, 1024), F32),
            pltpu.VMEM((BLOCK, REST), F32),
            pltpu.VMEM(SMALL, F32),
            DMA((7,)),
        ],
        compiler_params=pltpu.CompilerParams(vmem_limit_bytes=60 * 2**20),
    )(outs, outs_other, inner, inner_other, g1, g2, small))
    for n in (8, 12):
        results[n] = jnp.swapaxes(results[n], 1, 2)
    return tuple(results)


def solution(mesh):
    row, col = P("section", "ctx", "tp"), P("section", "tp", "ctx")
    gain, head = P("section", "ctx"), P("section", None)
    tokens = P(None, "ctx", None)
    layered = P("section", None, "ctx", None)
    return jax.shard_map(
        on_device,
        mesh=mesh,
        in_specs=(tokens, P(None, "ctx"), tokens, gain, row, row, row, head, head, col, gain, row, row, col),
        out_specs=(layered, layered, gain, row, row, row, head, head, col, gain, row, row, col),
        check_vma=False,
    )
```
